512 devices in a mesh: ctx: 16 (over x_lo, y), chan: 32 (over z, x_hi, core).
Axes of the slice: x: 4 (x_hi: 2, x_lo: 2; x = x_hi * 2 + x_lo), y: 8, z: 8, core: 2. Of those that a mesh axis runs over, the one named last changes fastest.
Arguments:
- query_proj: bfloat16 [8192, 4096], P('chan', 'ctx'), may hold values from -6 to 6
- key_proj: bfloat16 [8192, 4096], P('chan', 'ctx'), may hold values from -6 to 6
- value_proj: bfloat16 [8192, 4096], P('chan', 'ctx'), may hold values from -6 to 6
- out_cotangent: bfloat16 [8192, 4096], P('chan', 'ctx'), may hold values from -6 to 6
- short_taps: float32 [3, 7, 8192], P(None, None, 'chan'), may hold values from -2 to 2
- filter_in: float32 [33, 64], replicated, may hold values from -1 to 1
- filter_out: float32 [64, 8192], P(None, ('chan', 'ctx')), may hold values from -9 to 9
- decay_rate: float32 [8192], P(('chan', 'ctx')), may hold values from 0.5 to 400
- skip_gain: float32 [8192], P(('chan', 'ctx')), may hold values from -4 to 4
Outputs:
- mixed: bfloat16 [8192, 4096], P('chan', 'ctx')
- query_grad: bfloat16 [8192, 4096], P('chan', 'ctx')
- key_grad: bfloat16 [8192, 4096], P('chan', 'ctx')
- value_grad: bfloat16 [8192, 4096], P('chan', 'ctx')
- taps_grad: float32 [3, 7, 8192], P(None, None, 'chan')
- filter_in_grad: float32 [33, 64], replicated
- filter_out_grad: float32 [64, 8192], P(None, ('chan', 'ctx'))
- skip_grad: float32 [8192], P(('chan', 'ctx'))
The draws below stay inside these ranges and needn't reach their ends.
All inputs are finite; a program needn't handle non-finite values.
Results may differ from the reference program's by a relative error of at most 0.0057.
Values may be sent and summed in bfloat16 or wider, within the bound.
A program may use at most 64 MiB of HBM per device.

```python
import math
import jax
import jax.numpy as jnp
from jax import lax

D = 8192
FH = 64
EMB = 33
TAPS = 7
SEQ = 4096


def draw_filter_out(key, part):
    noise = jax.random.truncated_normal(key, -4.0, 4.0, (FH, D), jnp.float32)
    column = jnp.arange(D, dtype=jnp.float32) / max(D - 1, 1)
    rise = jnp.exp(column * math.log(3.0))[None, :]
    return noise * rise / math.sqrt(FH)


def draw_decay_rate(key, part):
    level = jax.random.uniform(key, (D,), jnp.float32)
    return jnp.exp(math.log(0.5) + level * math.log(800.0))


def block_scale(stream_key, dims, cuts, least, top_value):
    gain, own = 1.0, jax.random.fold_in(stream_key, 6)
    for axis_at, blocks in cuts:
        heights = jnp.exp(jax.random.uniform(jax.random.fold_in(own, axis_at), (blocks,), jnp.float32, least / len(cuts), top_value / len(cuts)))
        gain = gain * jnp.repeat(heights, dims[axis_at] // blocks).reshape([-1 if axis == axis_at else 1 for axis in range(len(dims))])
    return gain


def bell_draw(stream_key, shape, width, most, pieces=(), kind=jnp.bfloat16):
    drawn = jax.random.normal(stream_key, shape, jnp.float32) * width
    if len(pieces) > 0:
        drawn = block_scale(stream_key, shape, pieces, -0.22, 0.18) * drawn
    return jnp.clip(drawn, min=-most, max=most).astype(kind)


def setup_inputs(seed: int = 0) -> dict:
    key_list = jax.random.split(jax.random.key(seed), 10)
    query_proj = bell_draw(key_list[0], (D, SEQ), 1.0, 6.0, ((0, 32), (1, 16)))
    key_proj = bell_draw(key_list[1], (D, SEQ), 1.0, 6.0, ((0, 32), (1, 16)))
    value_proj = bell_draw(key_list[2], (D, SEQ), 1.0, 6.0, ((0, 32), (1, 16)))
    out_cotangent = bell_draw(key_list[3], (D, SEQ), 1.0, 6.0, ((0, 32), (1, 16)))
    short_taps = bell_draw(key_list[4], (3, TAPS, D), TAPS ** -0.5, 2.0, ((2, 32),), jnp.float32)
    filter_in = bell_draw(key_list[5], (EMB, FH), EMB ** -0.5, 1.0, (), jnp.float32)
    filter_out = draw_filter_out(jax.random.fold_in(key_list[9], 71), 0)
    decay_rate = draw_decay_rate(jax.random.fold_in(key_list[9], 71), 0)
    skip_gain = bell_draw(key_list[8], (D,), 1.0, 4.0, ((0, 512),), jnp.float32)
    return dict(query_proj=query_proj, key_proj=key_proj, value_proj=value_proj, out_cotangent=out_cotangent, short_taps=short_taps, filter_in=filter_in, filter_out=filter_out, decay_rate=decay_rate, skip_gain=skip_gain)


HIGH = lax.Precision.HIGHEST

def position_features(length, emb):
    bands = (emb - 1) // 2
    places = jnp.arange(length, dtype=jnp.int32)
    freqs = jnp.arange(1, bands + 1, dtype=jnp.int32)
    phase = (freqs[:, None] * places[None, :] % length).astype(jnp.float32) * (2.0 * math.pi / length)
    ramp = places.astype(jnp.float32)[None, :] / length
    return jnp.concatenate([ramp, jnp.cos(phase), jnp.sin(phase)], axis=0)

def reference(query_proj, key_proj, value_proj, out_cotangent, short_taps, filter_in, filter_out, decay_rate, skip_gain):
    block = math.gcd(D, 256)
    count = D // block
    reach = TAPS - 1
    scale = 1.0 / math.sqrt(SEQ)
    nfft = 2 * SEQ
    features = position_features(SEQ, EMB)
    pre = jnp.dot(filter_in.T, features, precision=HIGH, preferred_element_type=jnp.float32)
    act = jnp.sin(pre)
    bend = jnp.cos(pre)

    def one_block(index):
        start = index * block
        inputs = jnp.stack([lax.dynamic_slice_in_dim(query_proj, start, block, 0), lax.dynamic_slice_in_dim(key_proj, start, block, 0), lax.dynamic_slice_in_dim(value_proj, start, block, 0)]).astype(jnp.float32)
        cotan = lax.dynamic_slice_in_dim(out_cotangent, start, block, 0).astype(jnp.float32)
        taps = lax.dynamic_slice_in_dim(short_taps, start, block, 2)
        out_w = lax.dynamic_slice_in_dim(filter_out, start, block, 1)
        rate = lax.dynamic_slice_in_dim(decay_rate, start, block, 0)
        skip = lax.dynamic_slice_in_dim(skip_gain, start, block, 0)
        padded = jnp.pad(inputs, ((0, 0), (0, 0), (reach, 0)))
        shorts = jnp.zeros_like(inputs)
        for offset in range(TAPS):
            shorts = shorts + taps[:, offset, :, None] * padded[:, :, reach - offset:reach - offset + SEQ]
        q_short, k_short, v_short = (shorts[0], shorts[1], shorts[2])
        mixer_in = (k_short * v_short).astype(jnp.bfloat16)
        grad_in = (cotan * q_short).astype(jnp.bfloat16)
        envelope = jnp.exp(-rate[:, None] * features[0:1]) * scale
        raw = jnp.dot(out_w.T, act, precision=HIGH, preferred_element_type=jnp.float32)
        filt = raw * envelope
        mixer_f = mixer_in.astype(jnp.float32)
        grad_f = grad_in.astype(jnp.float32)
        spec_u = jnp.fft.rfft(mixer_f, n=nfft, axis=1)
        spec_h = jnp.fft.rfft(filt, n=nfft, axis=1)
        spec_g = jnp.fft.rfft(grad_f, n=nfft, axis=1)
        conv = jnp.fft.irfft(spec_u * spec_h, n=nfft, axis=1)[:, :SEQ] + skip[:, None] * mixer_f
        conv = conv.astype(jnp.bfloat16)
        mixed = (q_short * conv.astype(jnp.float32)).astype(jnp.bfloat16)
        back = jnp.fft.irfft(spec_g * jnp.conj(spec_h), n=nfft, axis=1)[:, :SEQ] + skip[:, None] * grad_f
        back = back.astype(jnp.bfloat16)
        filt_grad = jnp.fft.irfft(spec_g * jnp.conj(spec_u), n=nfft, axis=1)[:, :SEQ].astype(jnp.float32)
        skip_grad = lax.optimization_barrier(jnp.sum(grad_f * mixer_f, axis=1)) * scale
        bent = filt_grad * envelope
        out_grad = jnp.einsum('ft,ct->fc', act, bent, precision=HIGH) * scale
        act_grad = jnp.einsum('fc,ct->ft', out_w, bent, precision=HIGH)
        in_part = jnp.einsum('et,ft->ef', features, act_grad * bend, precision=HIGH)
        back_f = back.astype(jnp.float32)
        grads = jnp.stack([cotan * conv.astype(jnp.float32), back_f * v_short, back_f * k_short])
        extended = jnp.pad(grads, ((0, 0), (0, 0), (0, reach)))
        in_grads = jnp.zeros_like(grads)
        tap_list = []
        for offset in range(TAPS):
            in_grads = in_grads + taps[:, offset, :, None] * extended[:, :, offset:offset + SEQ]
            tap_list.append(lax.optimization_barrier(jnp.sum(grads * padded[:, :, reach - offset:reach - offset + SEQ], axis=2)) * scale)
        return (mixed, in_grads.astype(jnp.bfloat16), jnp.stack(tap_list, axis=1), out_grad, skip_grad, in_part)
    mixed, in_grads, tap_grads, out_grads, skip_grads, in_parts = lax.map(one_block, jnp.arange(count, dtype=jnp.int32))
    mixed = mixed.reshape(D, SEQ)
    in_grads = jnp.transpose(in_grads, (1, 0, 2, 3)).reshape(3, D, SEQ)
    tap_grads = jnp.transpose(tap_grads, (1, 2, 0, 3)).reshape(3, TAPS, D)
    out_grads = jnp.transpose(out_grads, (1, 0, 2)).reshape(FH, D)
    skip_grads = skip_grads.reshape(D)
    filter_in_grad = lax.optimization_barrier(jnp.sum(in_parts, axis=0)) * (scale / math.sqrt(D))
    return (mixed, in_grads[0], in_grads[1], in_grads[2], tap_grads, filter_in_grad, out_grads, skip_grads)
```

```python
import functools
import math

import jax
import jax.numpy as jnp
import ml_dtypes
import numpy as np
from jax import lax
from jax.experimental import pallas as pl
from jax.experimental.pallas import tpu as pltpu
from jax.sharding import PartitionSpec as P

D = 8192
SEQ = 4096
EMB = 33
FH = 64
TAPS = 7
NCTX = 16
POS = SEQ // NCTX
OWN = 16
K1 = 40
N1 = 64
N2 = 128
BLK = SEQ // N2
FEAT = 48
MESH = pl.DeviceIdType.MESH
f32 = jnp.float32
bf16 = jnp.bfloat16


def halves(x):
    x = np.asarray(x, np.float32)
    hi = x.astype(ml_dtypes.bfloat16)
    lo = (x - hi.astype(np.float32)).astype(ml_dtypes.bfloat16)
    return hi, lo


def tables():
    k1 = np.arange(K1)[:, None]
    live = (k1 <= N1 // 2).astype(np.float64)
    n = np.arange(BLK)[None, :]
    ang = 2 * np.pi * ((k1 * n) % N1) / N1
    c1 = np.concatenate([np.cos(ang) * live, -np.sin(ang) * live], 0)
    hi, lo = halves(c1)
    c1_two = np.concatenate([hi, lo], 1)
    c1_three = np.concatenate([hi, hi, lo], 1)
    weight = np.where((k1 == 0) | (k1 == N1 // 2), 1.0, 2.0) * live / (N1 * N2)
    d1 = np.concatenate([np.cos(ang) * weight, -np.sin(ang) * weight], 0).T
    hi, lo = halves(d1)
    d1_three = np.concatenate([hi, hi, lo], 1)
    m = np.arange(N2)
    turn = 2 * np.pi * ((m[:, None] * m[None, :]) % N2) / N2
    c, s = np.cos(turn), np.sin(turn)
    fwd = np.block([[c, -s], [s, c]])
    hi, lo = halves(fwd)
    fwd_three = np.concatenate([hi, hi, lo], 0)
    hi, lo = halves(fwd.T)
    inv_three = np.concatenate([hi, hi, lo], 0)
    twist = 2 * np.pi * ((k1 * m[None, :]) % (N1 * N2)) / (N1 * N2)
    twist = np.concatenate([np.cos(twist), np.sin(twist)], 0).astype(np.float32)
    t = np.arange(SEQ)
    bands = (EMB - 1) // 2
    b = np.arange(1, bands + 1)
    phase = 2 * np.pi * ((b[:, None] * t[None, :]) % SEQ) / SEQ
    feat = np.zeros((FEAT, SEQ))
    feat[0] = t / SEQ
    feat[1 : 1 + bands] = np.cos(phase)
    feat[1 + bands : 1 + 2 * bands] = np.sin(phase)
    feat_hi, feat_lo = halves(feat)
    tail = np.zeros((32, 3 * 128), np.float32)
    head = np.zeros((48, 6 * 128), np.float32)
    place = np.zeros((48, 3 * 128), np.float32)
    for i in range(3):
        for r in range(8):
            tail[i * 8 + r, i * 128 + 120 + r] = 1
            for h in range(2):
                head[i * 16 + h * 8 + r, (i * 2 + h) * 128 + r] = 1
                place[i * 16 + h * 8 + r, i * 128 + r] = 1
    as16 = lambda x: x.astype(ml_dtypes.bfloat16)
    return (c1_two, c1_three, d1_three, fwd_three, inv_three, twist, feat_hi, feat_lo,
            as16(tail), as16(head), as16(place))


def split(x):
    hi = x.astype(bf16)
    return hi, (x - hi.astype(f32)).astype(bf16)


def mm(a, b, ca=1, cb=0):
    return lax.dot_general(a, b, (((ca,), (cb,)), ((), ())), preferred_element_type=f32)


def sin_cos(x):
    n = jnp.floor(x * (1.0 / math.pi) + 0.5)
    r = x - n * 3.140625
    r = r - n * 9.67502593994140625e-4
    r = r - n * 1.509957990978376e-7
    sign = 1.0 - 2.0 * (n - 2.0 * jnp.floor(n * 0.5))
    z = r * r
    s = -1.0 / 39916800.0
    for k in (1.0 / 362880.0, -1.0 / 5040.0, 1.0 / 120.0, -1.0 / 6.0, 1.0):
        s = s * z + k
    c = 1.0 / 479001600.0
    for k in (-1.0 / 3628800.0, 1.0 / 40320.0, -1.0 / 720.0, 1.0 / 24.0, -0.5, 1.0):
        c = c * z + k
    return s * r * sign, c * sign


def kernel(quads, stacks,
           q_ref, k_ref, v_ref, cot_ref, taps_ref, fin_ref, fout_ref, decay_ref, skip_ref,
           c1_two, c1_three, d1_three, fwd_three, inv_three, twist, feat_hi, feat_lo,
           tail_sel, head_sel, head_place,
           mixed_ref, qg_ref, kg_ref, vg_ref, tg_ref, fig_ref, fog_ref, sg_ref,
           tails_out, tails_in, heads_out, heads_in, tap_rows, tap_cols, fin_pad,
           prev, shorts, shifted, grads, ahead, bend, act_hi, act_lo, env,
           sig, sig_u, spec_h, spec_u, spec_g,
           ug_out, ug_in, conv_out, conv_in, back_out, back_in, bent_hi, bent_lo,
           prods, tap_tiles, tap_parts, tap_sums, in_tiles, in_parts, in_mine,
           in_quad, in_next, in_stack, in_sums, in_flat,
           halo_s, halo_r, ug_s, ug_r, conv_s, conv_r, back_s, back_r,
           tp_s, tp_r, ts_s, ts_r, ip_s, ip_r, iq_s, iq_r, iz_s, iz_r, is_s, is_r):
    me = lax.axis_index("ctx")
    ch = lax.axis_index("chan")
    layer = ch // quads
    member = ch % quads

    def at(ctx_index):
        return {"ctx": ctx_index, "chan": ch}

    def over(chan_index):
        return {"ctx": me, "chan": chan_index}

    def copy(src, dst, send, recv, where):
        return pltpu.make_async_remote_copy(
            src_ref=src, dst_ref=dst, send_sem=send, recv_sem=recv,
            device_id=where, device_id_type=MESH)

    def each(count, body, start=1):
        def step(d, carry):
            body(d)
            return carry
        if count > start:
            lax.fori_loop(start, count, step, 0)

    def other(d):
        return lax.rem(me + d, NCTX)

    def quad_peer(d):
        return layer * quads + lax.rem(member + d, quads)

    def stack_peer(d):
        return lax.rem(layer + d, stacks) * quads + member

    barrier = pltpu.get_barrier_semaphore()

    def greet(where):
        pl.semaphore_signal(barrier, inc=1, device_id=where, device_id_type=MESH)

    each(NCTX, lambda d: greet(at(other(d))))
    each(quads, lambda d: greet(over(quad_peer(d))))
    each(stacks, lambda d: greet(over(stack_peer(d))))

    ends = jnp.concatenate([r[:, 128:256] for r in (q_ref, k_ref, v_ref)], axis=1)
    tails_out[...] = mm(tail_sel[...], ends, 1, 1).astype(bf16)
    pl.semaphore_wait(barrier, NCTX - 1 + (quads - 1) + (stacks - 1))
    tail_copy = copy(tails_out, tails_in, halo_s.at[0], halo_r.at[0], at(other(1)))
    tail_copy.start()

    tap_rows[...] = jnp.zeros_like(tap_rows)
    for i in range(3):
        tap_rows[i * 8 : i * 8 + TAPS, :] = taps_ref[i]
    row = lax.broadcasted_iota(jnp.int32, (24, 128), 0)
    col = lax.broadcasted_iota(jnp.int32, (24, 128), 1)
    unit = (row == col).astype(bf16)
    hi, lo = split(tap_rows[...])
    rest = (tap_rows[...] - hi.astype(f32) - lo.astype(f32)).astype(bf16)
    tap_cols[...] = mm(hi, unit, 0, 0) + mm(lo, unit, 0, 0) + mm(rest, unit, 0, 0)

    fin_pad[...] = jnp.zeros_like(fin_pad)
    fin_pad[0:EMB, :] = fin_ref[...]
    fin_hi, fin_lo = split(fin_pad[...])
    WIDE = 512

    def network(d):
        cols = pl.ds(pl.multiple_of(d * WIDE, WIDE), WIDE)
        a, b = feat_hi[:, cols], feat_lo[:, cols]
        pre = mm(fin_hi, a, 0, 0) + mm(fin_lo, a, 0, 0) + mm(fin_hi, b, 0, 0)
        s, c = sin_cos(pre)
        bend[:, cols] = c
        a, b = split(s)
        act_hi[:, cols] = a
        act_lo[:, cols] = b

    each(SEQ // WIDE, network, 0)

    tail_copy.wait_recv()
    inside = jnp.where(me > 0, 1.0, 0.0)
    prev[...] = mm(tails_in[...], tail_sel[...], 0, 0) * inside
    ROWS = 32
    CHUNKS = 256 // ROWS

    def moved(x, by):
        return x if by == 0 else pltpu.roll(x, by, 1)

    def short_part(d):
        part = lax.rem(me // 2 + d, CHUNKS)
        rows = pl.ds(pl.multiple_of(part * ROWS, ROWS), ROWS)
        res = []
        for i, ref in enumerate((q_ref, k_ref, v_ref)):
            x = jnp.concatenate(
                [prev[rows, i * 128 : (i + 1) * 128], ref[rows, :].astype(f32)], axis=1)
            acc = None
            for j in range(TAPS):
                term = tap_cols[rows, i * 8 + j : i * 8 + j + 1] * moved(x, j)[:, 128:384]
                acc = term if acc is None else acc + term
            shorts[i, rows, :] = acc
            res.append(acc)
        u = (res[1] * res[2]).astype(bf16)
        g = (cot_ref[rows, :].astype(f32) * res[0]).astype(bf16)
        for h in range(2):
            p = part * 2 + h
            ug_out[p, 0:16, :] = u[h * 16 : (h + 1) * 16, :]
            ug_out[p, 16:32, :] = g[h * 16 : (h + 1) * 16, :]

            @pl.when(p != me)
            def _():
                copy(ug_out.at[p], ug_in.at[me], ug_s.at[p], ug_r.at[me], at(p)).start()

    each(CHUNKS, short_part, 0)
    ug_in[me] = ug_out[me]

    eye = (lax.broadcasted_iota(jnp.int32, (OWN, OWN), 0)
           == lax.broadcasted_iota(jnp.int32, (OWN, OWN), 1)).astype(f32)
    decay = jnp.sum(eye * decay_ref[...], axis=1, keepdims=True)
    skip = jnp.sum(eye * skip_ref[...], axis=1, keepdims=True)
    w_hi, w_lo = split(fout_ref[...])
    scale = 1.0 / math.sqrt(SEQ)

    def filters(d):
        cols = pl.ds(pl.multiple_of(d * WIDE, WIDE), WIDE)
        a, b = act_hi[:, cols], act_lo[:, cols]
        raw = mm(w_hi, a, 0, 0) + mm(w_lo, a, 0, 0) + mm(w_hi, b, 0, 0)
        t = (d * WIDE + lax.broadcasted_iota(jnp.int32, (OWN, WIDE), 1)).astype(f32)
        e = jnp.exp(-decay * (t * (1.0 / SEQ))) * scale
        h = raw * e
        for n in range(WIDE // 128):
            rows = pl.ds(pl.multiple_of((d * (WIDE // 128) + n) * OWN, OWN), OWN)
            env[rows, :] = e[:, n * 128 : (n + 1) * 128]
            sig[rows, :] = h[:, n * 128 : (n + 1) * 128]

    each(SEQ // WIDE, filters, 0)

    GRP = 4
    tc, ts = twist[0:K1, :], twist[K1 : 2 * K1, :]

    def three(x, axis):
        hi, lo = split(x)
        return jnp.concatenate([hi, lo, hi], axis=axis)

    def forward(src, spec, exact):
        for grp in range(OWN // GRP):
            x = jnp.concatenate(
                [src[pl.ds(grp * GRP + c, BLK, stride=OWN), :] for c in range(GRP)], axis=1)
            if exact:
                x = x.astype(bf16)
                a = mm(c1_two[...], jnp.concatenate([x, x], axis=0))
            else:
                a = mm(c1_three[...], three(x, 0))
            re, im = [], []
            for c in range(GRP):
                ar = a[0:K1, c * 128 : (c + 1) * 128]
                ai = a[K1 : 2 * K1, c * 128 : (c + 1) * 128]
                re.append(ar * tc + ai * ts)
                im.append(ai * tc - ar * ts)
            x = jnp.concatenate([jnp.concatenate(re, 0), jnp.concatenate(im, 0)], axis=1)
            spec[grp * GRP * K1 : (grp + 1) * GRP * K1, :] = mm(three(x, 1), fwd_three[...])

    def backward(first, second, conj, dst):
        for grp in range(OWN // GRP):
            rows = slice(grp * GRP * K1, (grp + 1) * GRP * K1)
            ar, ai = first[rows, 0:128], first[rows, 128:256]
            br, bi = second[rows, 0:128], second[rows, 128:256]
            if conj:
                y = [ar * br + ai * bi, ai * br - ar * bi]
            else:
                y = [ar * br - ai * bi, ar * bi + ai * br]
            z = mm(three(jnp.concatenate(y, axis=1), 1), inv_three[...])
            out = []
            for c in range(GRP):
                zr = z[c * K1 : (c + 1) * K1, 0:128]
                zi = z[c * K1 : (c + 1) * K1, 128:256]
                out.append(jnp.concatenate([zr * tc - zi * ts, zi * tc + zr * ts], axis=0))
            r = mm(d1_three[...], three(jnp.concatenate(out, axis=1), 0))
            for c in range(GRP):
                dst[pl.ds(grp * GRP + c, BLK, stride=OWN), :] = r[:, c * 128 : (c + 1) * 128]

    forward(sig, spec_h, False)

    def shift_part(d):
        rows = pl.ds(pl.multiple_of(d * ROWS, ROWS), ROWS)
        for i, ref in enumerate((q_ref, k_ref, v_ref)):
            x = jnp.concatenate(
                [prev[rows, i * 128 : (i + 1) * 128], ref[rows, :].astype(f32)], axis=1)
            for j in range(TAPS):
                shifted[i * TAPS + j, rows, :] = moved(x, j)[:, 128:384].astype(bf16)

    each(CHUNKS, shift_part, 0)

    def ug_wait(d):
        p = other(d)
        copy(ug_out.at[p], ug_in.at[p], ug_s.at[p], ug_r.at[p], at(p)).wait_recv()

    each(NCTX, ug_wait)
    for s in range(NCTX):
        for h in range(2):
            n = 2 * s + h
            sig_u[n * 16 : (n + 1) * 16, :] = ug_in[s, 0:16, h * 128 : (h + 1) * 128].astype(f32)
            sig[n * 16 : (n + 1) * 16, :] = ug_in[s, 16:32, h * 128 : (h + 1) * 128].astype(f32)
    forward(sig_u, spec_u, True)
    forward(sig, spec_g, True)

    def scatter(result, first_row, out, inn, send, recv):
        for s in range(NCTX):
            x = jnp.concatenate(
                [result[(2 * s + h) * 16 : (2 * s + h + 1) * 16, :] for h in range(2)], axis=1)
            x = x + skip * ug_in[s, first_row : first_row + 16, :].astype(f32)
            out[s] = x.astype(bf16)
        mine = pl.ds(pl.multiple_of(me * 16, 16), 16)
        inn[mine, :] = out[me]

        def go(d):
            p = other(d)
            copy(out.at[p], inn.at[mine, :], send.at[p], recv.at[me], at(p)).start()

        each(NCTX, go)

    backward(spec_u, spec_h, False, sig_u)
    scatter(sig_u, 0, conv_out, conv_in, conv_s, conv_r)
    backward(spec_g, spec_h, True, sig)
    scatter(sig, 16, back_out, back_in, back_s, back_r)

    backward(spec_g, spec_u, True, sig)
    sg_ref[...] = jnp.sum(eye * sig[0:16, 0:1], axis=0, keepdims=True) * scale
    for n in range(BLK):
        a, b = split(sig[n * 16 : (n + 1) * 16, :] * env[n * 16 : (n + 1) * 16, :])
        bent_hi[:, n * 128 : (n + 1) * 128] = a
        bent_lo[:, n * 128 : (n + 1) * 128] = b

    def gradient(d, carry):
        out_sum, in_sum = carry
        cols = pl.ds(pl.multiple_of(d * WIDE, WIDE), WIDE)
        bh, bl = bent_hi[:, cols], bent_lo[:, cols]
        ah, al = act_hi[:, cols], act_lo[:, cols]
        out_sum = out_sum + mm(ah, bh, 1, 1) + mm(al, bh, 1, 1) + mm(ah, bl, 1, 1)
        slope = (mm(w_hi, bh) + mm(w_lo, bh) + mm(w_hi, bl)) * bend[:, cols]
        sh, sl = split(slope)
        fh, fl = feat_hi[:, cols], feat_lo[:, cols]
        in_sum = in_sum + mm(fh, sh, 1, 1) + mm(fl, sh, 1, 1) + mm(fh, sl, 1, 1)
        return out_sum, in_sum

    out_sum, in_sum = lax.fori_loop(
        0, SEQ // WIDE, gradient, (jnp.zeros((FH, OWN), f32), jnp.zeros((FEAT, FH), f32)))
    fog_ref[...] = out_sum * scale
    in_flat[...] = jnp.zeros_like(in_flat)
    in_flat[:, 0:FH] = in_sum
    packed = in_flat[0:24, :] + pltpu.roll(in_flat[24:48, :], 64, 1)
    for k in range(3):
        in_tiles[k] = packed[k * 8 : (k + 1) * 8, :]

    def deal(count, odd, tiles, parts, send, recv, go):
        for k in range(count):
            @pl.when(me != 2 * k + odd)
            def _(k=k):
                c = copy(tiles.at[k], parts.at[me], send.at[k], recv.at[me], at(2 * k + odd))
                go(c)

    deal(3, 1, in_tiles, in_parts, ip_s, ip_r, lambda c: c.start())
    in_owner = jnp.logical_and(lax.rem(me, 2) == 1, me < 6)
    tap_owner = jnp.logical_and(lax.rem(me, 2) == 0, me < 12)
    in_index = jnp.minimum(me // 2, 2)
    tap_index = jnp.minimum(me // 2, 5)

    def rows_wait(out, inn, send, recv):
        def one(d):
            p = other(d)
            rows = pl.ds(pl.multiple_of(p * 16, 16), 16)
            copy(out.at[p], inn.at[rows, :], send.at[p], recv.at[p], at(p)).wait_recv()
        each(NCTX, one)

    rows_wait(conv_out, conv_in, conv_s, conv_r)
    rows_wait(back_out, back_in, back_s, back_r)

    def grad_part(d):
        rows = pl.ds(pl.multiple_of(d * ROWS, ROWS), ROWS)
        cv = conv_in[rows, :].astype(f32)
        bk = back_in[rows, :].astype(f32)
        mixed_ref[rows, :] = (shorts[0, rows, :] * cv).astype(bf16)
        gs = (cot_ref[rows, :].astype(f32) * cv, bk * shorts[2, rows, :], bk * shorts[1, rows, :])
        for i in range(3):
            grads[i, rows, :] = gs[i]
            hi, lo = split(gs[i][:, 0:128])
            ahead[rows, i * 256 : i * 256 + 128] = hi
            ahead[rows, i * 256 + 128 : i * 256 + 256] = lo

    each(CHUNKS, grad_part, 0)
    heads_out[...] = mm(head_sel[...], ahead[...], 1, 1).astype(bf16)
    head_copy = copy(heads_out, heads_in, halo_s.at[1], halo_r.at[1], at(other(NCTX - 1)))
    head_copy.start()

    def collect(parts, tiles, index, recv, sender_count):
        def one(d):
            p = other(d)
            copy(tiles.at[0], parts.at[p], recv.at[p], recv.at[p], at(p)).wait_recv()
        each(NCTX, one)
        parts[me] = tiles[index]
        total = parts[0]
        for p in range(1, sender_count):
            total = total + parts[p]
        return total

    @pl.when(in_owner)
    def _():
        in_quad[member] = collect(in_parts, in_tiles, in_index, ip_r, NCTX)

        def go(d):
            p = quad_peer(d)
            copy(in_quad.at[member], in_quad.at[member], iq_s.at[d], iq_r.at[member],
                 over(p)).start()
        each(quads, go)

    def prod_part(d):
        rows = pl.ds(pl.multiple_of(d * ROWS, ROWS), ROWS)
        for i in range(3):
            g = grads[i, rows, :]
            for j in range(TAPS):
                x = g * shifted[i * TAPS + j, rows, :].astype(f32)
                hi, lo = split(x[:, 0:128] + x[:, 128:256])
                prods[i * TAPS + j, rows, 0:128] = hi
                prods[i * TAPS + j, rows, 128:256] = lo

    each(CHUNKS, prod_part, 0)
    pick_row = lax.broadcasted_iota(jnp.int32, (32, 256), 0)
    total = jnp.zeros((32, 256), f32)
    for i in range(3):
        for j in range(TAPS):
            pick = (pick_row == i * 8 + j).astype(f32).astype(bf16)
            total = total + mm(pick, prods[i * TAPS + j], 1, 1)
    for k in range(6):
        tap_tiles[k] = total[(k // 2) * 8 : (k // 2) * 8 + 8, (k % 2) * 128 : (k % 2) * 128 + 128]
    deal(6, 0, tap_tiles, tap_parts, tp_s, tp_r, lambda c: c.start())

    @pl.when(in_owner)
    def _():
        def one(d):
            p = lax.rem(member + d, quads)
            copy(in_quad.at[p], in_quad.at[p], iq_s.at[d], iq_r.at[p], over(quad_peer(d))).wait_recv()
        each(quads, one)
        t = in_quad[0]
        for p in range(1, quads):
            t = t + in_quad[p]
        in_stack[layer] = t

        def go(d):
            copy(in_stack.at[layer], in_stack.at[layer], iz_s.at[d], iz_r.at[layer],
                 over(stack_peer(d))).start()
        each(stacks, go)

    head_copy.wait_recv()
    before_end = jnp.where(me < NCTX - 1, 1.0, 0.0)
    prev[...] = mm(heads_in[...], head_place[...], 0, 0) * before_end

    def proj_part(d):
        rows = pl.ds(pl.multiple_of(d * ROWS, ROWS), ROWS)
        for i, ref in enumerate((qg_ref, kg_ref, vg_ref)):
            x = jnp.concatenate([grads[i, rows, :], prev[rows, i * 128 : (i + 1) * 128]], axis=1)
            acc = None
            for j in range(TAPS):
                y = moved(x, (384 - j) % 384)[:, 0:256]
                term = tap_cols[rows, i * 8 + j : i * 8 + j + 1] * y
                acc = term if acc is None else acc + term
            ref[rows, :] = acc.astype(bf16)

    each(CHUNKS, proj_part, 0)

    @pl.when(tap_owner)
    def _():
        tap_sums[tap_index] = collect(tap_parts, tap_tiles, tap_index, tp_r, NCTX)

        def go(d):
            copy(tap_sums.at[tap_index], tap_sums.at[tap_index], ts_s.at[d], ts_r.at[tap_index],
                 at(other(d))).start()
        each(NCTX, go)

    @pl.when(in_owner)
    def _():
        def one(d):
            p = lax.rem(layer + d, stacks)
            copy(in_stack.at[p], in_stack.at[p], iz_s.at[d], iz_r.at[p], over(stack_peer(d))).wait_recv()
        each(stacks, one)
        t = in_stack[0]
        for p in range(1, stacks):
            t = t + in_stack[p]
        in_sums[in_index] = t

        def go(d):
            copy(in_sums.at[in_index], in_sums.at[in_index], is_s.at[d], is_r.at[in_index],
                 at(other(d))).start()
        each(NCTX, go)

    for k in range(6):
        @pl.when(me != 2 * k)
        def _(k=k):
            copy(tap_sums.at[k], tap_sums.at[k], ts_s.at[0], ts_r.at[k], at(2 * k)).wait_recv()
    for i in range(3):
        both = jnp.concatenate([tap_sums[2 * i], tap_sums[2 * i + 1]], axis=1) * scale
        tg_ref[i] = both[0:TAPS, :]
    for k in range(3):
        @pl.when(me != 2 * k + 1)
        def _(k=k):
            copy(in_sums.at[k], in_sums.at[k], is_s.at[0], is_r.at[k], at(2 * k + 1)).wait_recv()
    sums = jnp.concatenate([in_sums[k] for k in range(3)], axis=0) * (scale / math.sqrt(D))
    fig_ref[0:24, :] = sums[:, 0:FH]
    fig_ref[24:EMB, :] = pltpu.roll(sums, 64, 1)[0 : EMB - 24, 0:FH]

    tail_copy.wait_send()
    head_copy.wait_send()
    deal(3, 1, in_tiles, in_parts, ip_s, ip_r, lambda c: c.wait_send())
    deal(6, 0, tap_tiles, tap_parts, tp_s, tp_r, lambda c: c.wait_send())

    def left(d):
        p = other(d)
        mine = pl.ds(pl.multiple_of(me * 16, 16), 16)
        copy(ug_out.at[p], ug_in.at[me], ug_s.at[p], ug_r.at[me], at(p)).wait_send()
        copy(conv_out.at[p], conv_in.at[mine, :], conv_s.at[p], conv_r.at[me], at(p)).wait_send()
        copy(back_out.at[p], back_in.at[mine, :], back_s.at[p], back_r.at[me], at(p)).wait_send()

    each(NCTX, left)

    @pl.when(in_owner)
    def _():
        each(quads, lambda d: copy(in_quad.at[member], in_quad.at[member], iq_s.at[d],
                                   iq_r.at[member], over(quad_peer(d))).wait_send())
        each(stacks, lambda d: copy(in_stack.at[layer], in_stack.at[layer], iz_s.at[d],
                                    iz_r.at[layer], over(stack_peer(d))).wait_send())
        each(NCTX, lambda d: copy(in_sums.at[in_index], in_sums.at[in_index], is_s.at[d],
                                  is_r.at[in_index], at(other(d))).wait_send())

    @pl.when(tap_owner)
    def _():
        each(NCTX, lambda d: copy(tap_sums.at[tap_index], tap_sums.at[tap_index], ts_s.at[d],
                                  ts_r.at[tap_index], at(other(d))).wait_send())


def per_device(consts, chans, query_proj, key_proj, value_proj, out_cotangent, short_taps,
               filter_in, filter_out, decay_rate, skip_gain):
    quads = math.gcd(chans, 4)
    stacks = chans // quads
    vm = pl.BlockSpec(memory_space=pltpu.VMEM)
    block = jax.ShapeDtypeStruct((256, POS), bf16)
    dma = pltpu.SemaphoreType.DMA
    V = pltpu.VMEM
    args = (query_proj, key_proj, value_proj, out_cotangent, short_taps, filter_in, filter_out,
            decay_rate.reshape(1, OWN), skip_gain.reshape(1, OWN))
    outs = pl.pallas_call(
        functools.partial(kernel, quads, stacks),
        out_shape=(block, block, block, block,
                   jax.ShapeDtypeStruct((3, TAPS, 256), f32),
                   jax.ShapeDtypeStruct((EMB, FH), f32),
                   jax.ShapeDtypeStruct((FH, OWN), f32),
                   jax.ShapeDtypeStruct((1, OWN), f32)),
        in_specs=[vm] * (len(args) + len(consts)),
        out_specs=[vm] * 8,
        scratch_shapes=[
            V((32, 256), bf16), V((32, 256), bf16), V((48, 256), bf16), V((48, 256), bf16),
            V((24, 256), f32), V((256, 128), f32), V((FEAT, FH), f32),
            V((256, 384), f32), V((3, 256, 256), f32), V((21, 256, 256), bf16),
            V((3, 256, 256), f32), V((256, 768), bf16), V((FH, SEQ), f32),
            V((FH, SEQ), bf16), V((FH, SEQ), bf16), V((512, 128), f32),
            V((512, 128), f32), V((512, 128), f32),
            V((OWN * K1, 256), f32), V((OWN * K1, 256), f32), V((OWN * K1, 256), f32),
            V((NCTX, 32, 256), bf16), V((NCTX, 32, 256), bf16),
            V((NCTX, 16, 256), bf16), V((256, 256), bf16),
            V((NCTX, 16, 256), bf16), V((256, 256), bf16),
            V((OWN, SEQ), bf16), V((OWN, SEQ), bf16),
            V((21, 256, 256), bf16), V((6, 8, 128), f32), V((NCTX, 8, 128), f32),
            V((6, 8, 128), f32),
            V((3, 8, 128), f32), V((NCTX, 8, 128), f32), V((8, 128), f32),
            V((quads, 8, 128), f32), V((8, 128), f32), V((stacks, 8, 128), f32),
            V((3, 8, 128), f32), V((48, 128), f32),
            dma((2,)), dma((2,)), dma((NCTX,)), dma((NCTX,)),
            dma((NCTX,)), dma((NCTX,)), dma((NCTX,)), dma((NCTX,)),
            dma((6,)), dma((NCTX,)), dma((NCTX,)), dma((6,)),
            dma((3,)), dma((NCTX,)), dma((quads,)), dma((quads,)),
            dma((stacks,)), dma((stacks,)), dma((NCTX,)), dma((3,)),
        ],
        compiler_params=pltpu.CompilerParams(
            collective_id=0, has_side_effects=True, vmem_limit_bytes=56 * 1024 * 1024),
    )(*args, *[jnp.asarray(c) for c in consts])
    return outs[:7] + (outs[7].reshape(OWN),)


def solution(mesh):
    consts = tables()
    return jax.shard_map(
        functools.partial(per_device, consts, mesh.shape["chan"]),
        mesh=mesh,
        in_specs=(
            P("chan", "ctx"),
            P("chan", "ctx"),
            P("chan", "ctx"),
            P("chan", "ctx"),
            P(None, None, "chan"),
            P(),
            P(None, ("chan", "ctx")),
            P(("chan", "ctx")),
            P(("chan", "ctx")),
        ),
        out_specs=(
            P("chan", "ctx"),
            P("chan", "ctx"),
            P("chan", "ctx"),
            P("chan", "ctx"),
            P(None, None, "chan"),
            P(),
            P(None, ("chan", "ctx")),
            P(("chan", "ctx")),
        ),
        check_vma=False,
    )
```

```python
import functools
import math

import jax
import jax.numpy as jnp
import ml_dtypes
import numpy as np
from jax import lax
from jax.experimental import pallas as pl
from jax.experimental.pallas import tpu as pltpu
from jax.sharding import PartitionSpec as P

D = 8192
SEQ = 4096
EMB = 33
FH = 64
TAPS = 7
NCTX = 16
POS = SEQ // NCTX
OWN = 16
K1 = 40
N1 = 64
N2 = 128
BLK = SEQ // N2
FEAT = 48
LOADS = 19
MESH = pl.DeviceIdType.MESH
f32 = jnp.float32
bf16 = jnp.bfloat16


def halves(x):
    x = np.asarray(x, np.float32)
    hi = x.astype(ml_dtypes.bfloat16)
    lo = (x - hi.astype(np.float32)).astype(ml_dtypes.bfloat16)
    return hi, lo


def tables():
    k1 = np.arange(K1)[:, None]
    live = (k1 <= N1 // 2).astype(np.float64)
    n = np.arange(BLK)[None, :]
    ang = 2 * np.pi * ((k1 * n) % N1) / N1
    c1 = np.concatenate([np.cos(ang) * live, -np.sin(ang) * live], 0)
    hi, lo = halves(c1)
    c1_two = np.concatenate([hi, lo], 1)
    c1_three = np.concatenate([hi, hi, lo], 1)
    weight = np.where((k1 == 0) | (k1 == N1 // 2), 1.0, 2.0) * live / (N1 * N2)
    d1 = np.concatenate([np.cos(ang) * weight, -np.sin(ang) * weight], 0).T
    hi, lo = halves(d1)
    d1_three = np.concatenate([hi, hi, lo], 1)
    m = np.arange(N2)
    turn = 2 * np.pi * ((m[:, None] * m[None, :]) % N2) / N2
    c, s = np.cos(turn), np.sin(turn)
    fwd = np.block([[c, -s], [s, c]])
    hi, lo = halves(fwd)
    fwd_three = np.concatenate([hi, hi, lo], 0)
    hi, lo = halves(fwd.T)
    inv_three = np.concatenate([hi, hi, lo], 0)
    twist = 2 * np.pi * ((k1 * m[None, :]) % (N1 * N2)) / (N1 * N2)
    twist = np.concatenate([np.cos(twist), np.sin(twist)], 0).astype(np.float32)
    t = np.arange(SEQ)
    bands = (EMB - 1) // 2
    b = np.arange(1, bands + 1)
    phase = 2 * np.pi * ((b[:, None] * t[None, :]) % SEQ) / SEQ
    feat = np.zeros((FEAT, SEQ))
    feat[0] = t / SEQ
    feat[1 : 1 + bands] = np.cos(phase)
    feat[1 + bands : 1 + 2 * bands] = np.sin(phase)
    feat_two = np.concatenate(halves(feat), 0)
    tail = np.zeros((32, 3 * 128), np.float32)
    head = np.zeros((48, 6 * 128), np.float32)
    place = np.zeros((48, 18 * 128), np.float32)
    for i in range(3):
        for r in range(8):
            tail[i * 8 + r, i * 128 + 120 + r] = 1
            for h in range(2):
                head[i * 16 + h * 8 + r, (i * 2 + h) * 128 + r] = 1
                for j in range(r + 1, TAPS):
                    place[i * 16 + h * 8 + r, (i * 6 + j - 1) * 128 + 128 + r - j] = 1
    as16 = lambda x: x.astype(ml_dtypes.bfloat16)
    return (c1_two, c1_three, d1_three, fwd_three, inv_three, twist, feat_two,
            as16(tail), as16(head), as16(place))


def split(x):
    hi = x.astype(bf16)
    return hi, (x - hi.astype(f32)).astype(bf16)


def mm(a, b, ca=1, cb=0):
    return lax.dot_general(a, b, (((ca,), (cb,)), ((), ())), preferred_element_type=f32)


def sin_cos(x):
    n = jnp.floor(x * (1.0 / math.pi) + 0.5)
    r = x - n * 3.140625
    r = r - n * 9.67502593994140625e-4
    r = r - n * 1.509957990978376e-7
    sign = 1.0 - 2.0 * (n - 2.0 * jnp.floor(n * 0.5))
    z = r * r
    s = -1.0 / 39916800.0
    for k in (1.0 / 362880.0, -1.0 / 5040.0, 1.0 / 120.0, -1.0 / 6.0, 1.0):
        s = s * z + k
    c = 1.0 / 479001600.0
    for k in (-1.0 / 3628800.0, 1.0 / 40320.0, -1.0 / 720.0, 1.0 / 24.0, -0.5, 1.0):
        c = c * z + k
    return s * r * sign, c * sign


def kernel(quads, stacks,
           *refs):
    sources, refs = refs[:LOADS], refs[LOADS:]
    targets, refs = refs[:8], refs[8:]
    held, refs = refs[:LOADS], refs[LOADS:]
    done, refs = refs[:8], refs[8:]
    (q_ref, k_ref, v_ref, cot_ref, taps_ref, fin_ref, fout_ref, decay_ref, skip_ref,
     c1_two, c1_three, d1_three, fwd_three, inv_three, twist, feat,
     tail_sel, head_sel, head_place) = held
    mixed_ref, qg_ref, kg_ref, vg_ref, tg_ref, fig_ref, fog_ref, sg_ref = done
    (load_s, store_s, tails_out, tails_in, heads_out, heads_in, tap_rows, tap_cols, fin_pad,
     tap_wide, prev, after, shorts, shifted, grads, ahead, bend, act, env,
     sig, sig_u, spec_h, spec_u, spec_g,
     ug_out, ug_in, conv_out, conv_in, back_out, back_in, bent, slope,
     prods, tap_tiles, tap_parts, tap_sums, in_tiles, in_parts,
     in_quad, in_stack, in_sums, in_flat,
     halo_s, halo_r, ug_s, ug_r, conv_s, conv_r, back_s, back_r,
     tp_s, tp_r, ts_s, ts_r, ip_s, ip_r, iq_s, iq_r, iz_s, iz_r, is_s, is_r) = refs
    me = lax.axis_index("ctx")
    ch = lax.axis_index("chan")
    layer = ch // quads
    member = ch % quads

    def at(ctx_index):
        return {"ctx": ctx_index, "chan": ch}

    def over(chan_index):
        return {"ctx": me, "chan": chan_index}

    def copy(src, dst, send, recv, where):
        return pltpu.make_async_remote_copy(
            src_ref=src, dst_ref=dst, send_sem=send, recv_sem=recv,
            device_id=where, device_id_type=MESH)

    def each(count, body, start=1):
        for d in range(start, count):
            body(d)

    def other(d):
        return lax.rem(me + d, NCTX)

    def quad_peer(d):
        return layer * quads + lax.rem(member + d, quads)

    def stack_peer(d):
        return lax.rem(layer + d, stacks) * quads + member

    barrier = pltpu.get_barrier_semaphore()

    def greet(where):
        pl.semaphore_signal(barrier, inc=1, device_id=where, device_id_type=MESH)

    each(NCTX, lambda d: greet(at(other(d))))
    each(quads, lambda d: greet(over(quad_peer(d))))
    each(stacks, lambda d: greet(over(stack_peer(d))))

    def load(k):
        return pltpu.make_async_copy(sources[k], held[k], load_s.at[k])

    def store(k):
        return pltpu.make_async_copy(done[k], targets[k], store_s.at[k])

    for k in (0, 1, 2, 16, 4, 5, 15, 3, 6, 7, 8, 14, 10, 12, 9, 11, 13, 17, 18):
        load(k).start()

    for k in (0, 1, 2, 16):
        load(k).wait()
    ends = jnp.concatenate([r[:, 128:256] for r in (q_ref, k_ref, v_ref)], axis=1)
    tails_out[...] = mm(tail_sel[...], ends, 1, 1).astype(bf16)
    pl.semaphore_wait(barrier, NCTX - 1 + (quads - 1) + (stacks - 1))
    tail_copy = copy(tails_out, tails_in, halo_s.at[0], halo_r.at[0], at(other(1)))
    tail_copy.start()

    load(4).wait()
    tap_rows[...] = jnp.zeros_like(tap_rows)
    for i in range(3):
        tap_rows[i * 8 : i * 8 + TAPS, :] = taps_ref[i]
    row = lax.broadcasted_iota(jnp.int32, (24, 128), 0)
    col = lax.broadcasted_iota(jnp.int32, (24, 128), 1)
    unit = (row == col).astype(bf16)
    hi, lo = split(tap_rows[...])
    rest = (tap_rows[...] - hi.astype(f32) - lo.astype(f32)).astype(bf16)
    tap_cols[...] = mm(hi, unit, 0, 0) + mm(lo, unit, 0, 0) + mm(rest, unit, 0, 0)
    ROWS = 32
    CHUNKS = 256 // ROWS

    def spread(d):
        rows = pl.ds(d * ROWS, ROWS)
        for i in range(3):
            for j in range(TAPS):
                one = tap_cols[rows, i * 8 + j : i * 8 + j + 1]
                tap_wide[i * TAPS + j, rows, :] = jnp.broadcast_to(one, (ROWS, 128))

    each(CHUNKS, spread, 0)

    load(5).wait()
    load(15).wait()
    fin_pad[...] = jnp.zeros_like(fin_pad)
    fin_pad[0:EMB, :] = fin_ref[...]
    fin_hi, fin_lo = split(fin_pad[...])
    fin_three = jnp.concatenate([fin_hi, fin_hi, fin_lo], axis=0)
    WIDE = 512

    def network(d):
        cols = pl.ds(d * WIDE, WIDE)
        f = feat[:, cols]
        pre = mm(fin_three, jnp.concatenate([f, f[0:FEAT, :]], axis=0), 0, 0)
        s, c = sin_cos(pre)
        bend[:, cols] = c
        a, b = split(s)
        act[0:FH, cols] = a
        act[FH : 2 * FH, cols] = b

    each(SEQ // WIDE, network, 0)

    load(3).wait()
    tail_copy.wait_recv()
    inside = jnp.where(me > 0, 1.0, 0.0)
    prev[...] = (mm(tails_in[...], tail_sel[...], 0, 0) * inside).astype(bf16)

    def moved(x, by):
        return x if by == 0 else pltpu.roll(x, by, 1)

    def short_part(d):
        part = lax.rem(me // 2 + d, CHUNKS)
        rows = pl.ds(pl.multiple_of(part * ROWS, ROWS), ROWS)
        res = []
        for i, ref in enumerate((q_ref, k_ref, v_ref)):
            x = jnp.concatenate([prev[rows, i * 128 : (i + 1) * 128], ref[rows, :]], axis=1)
            acc = None
            for j in range(TAPS):
                y = moved(x, j)[:, 128:384]
                shifted[i * TAPS + j, rows, :] = y
                tap = tap_wide[i * TAPS + j, rows, :]
                term = jnp.concatenate([tap, tap], axis=1) * y.astype(f32)
                acc = term if acc is None else acc + term
            shorts[i, rows, :] = acc
            res.append(acc)
        u = (res[1] * res[2]).astype(bf16)
        g = (cot_ref[rows, :].astype(f32) * res[0]).astype(bf16)
        for h in range(2):
            p = part * 2 + h
            ug_out[p, 0:16, :] = u[h * 16 : (h + 1) * 16, :]
            ug_out[p, 16:32, :] = g[h * 16 : (h + 1) * 16, :]
        mate = part * 2 + 1 - lax.rem(me, 2)
        for p in ((mate,) if d == 0 else (part * 2, part * 2 + 1)):
            copy(ug_out.at[p], ug_in.at[me], ug_s.at[p], ug_r.at[me], at(p)).start()

    each(CHUNKS, short_part, 0)
    ug_in[me] = ug_out[me]

    for k in (6, 7, 8):
        load(k).wait()
    eye = (lax.broadcasted_iota(jnp.int32, (OWN, OWN), 0)
           == lax.broadcasted_iota(jnp.int32, (OWN, OWN), 1)).astype(f32)
    decay = jnp.sum(eye * decay_ref[...], axis=1, keepdims=True)
    skip = jnp.sum(eye * skip_ref[...], axis=1, keepdims=True)
    w_hi, w_lo = split(fout_ref[...])
    w_two = jnp.concatenate([w_hi, w_lo], axis=0)
    w_three = jnp.concatenate([w_hi, w_hi, w_lo], axis=0)
    scale = 1.0 / math.sqrt(SEQ)

    def filters(d):
        cols = pl.ds(d * WIDE, WIDE)
        raw = mm(w_two, act[0:FH, cols])
        raw = raw[0:OWN, :] + raw[OWN : 2 * OWN, :] + mm(w_hi, act[FH : 2 * FH, cols])
        t = (d * WIDE + lax.broadcasted_iota(jnp.int32, (OWN, WIDE), 1)).astype(f32)
        e = jnp.exp(-decay * (t * (1.0 / SEQ))) * scale
        h = raw * e
        for n in range(WIDE // 128):
            rows = pl.ds((d * (WIDE // 128) + n) * OWN, OWN)
            env[rows, :] = e[:, n * 128 : (n + 1) * 128]
            sig[rows, :] = h[:, n * 128 : (n + 1) * 128]

    each(SEQ // WIDE, filters, 0)

    for k in (9, 10, 11, 12, 13, 14):
        load(k).wait()
    GRP = 4
    tc, ts = twist[0:K1, :], twist[K1 : 2 * K1, :]

    def three(x, axis):
        hi, lo = split(x)
        return jnp.concatenate([hi, lo, hi], axis=axis)

    def forward(src, spec, exact):
        for grp in range(OWN // GRP):
            x = jnp.concatenate(
                [src[pl.ds(grp * GRP + c, BLK, stride=OWN), :] for c in range(GRP)], axis=1)
            if exact:
                x = x.astype(bf16)
                a = mm(c1_two[...], jnp.concatenate([x, x], axis=0))
            else:
                a = mm(c1_three[...], three(x, 0))
            re, im = [], []
            for c in range(GRP):
                ar = a[0:K1, c * 128 : (c + 1) * 128]
                ai = a[K1 : 2 * K1, c * 128 : (c + 1) * 128]
                re.append(ar * tc + ai * ts)
                im.append(ai * tc - ar * ts)
            x = jnp.concatenate([jnp.concatenate(re, 0), jnp.concatenate(im, 0)], axis=1)
            spec[grp * GRP * K1 : (grp + 1) * GRP * K1, :] = mm(three(x, 1), fwd_three[...])

    def backward(first, second, conj, dst):
        for grp in range(OWN // GRP):
            rows = slice(grp * GRP * K1, (grp + 1) * GRP * K1)
            ar, ai = first[rows, 0:128], first[rows, 128:256]
            br, bi = second[rows, 0:128], second[rows, 128:256]
            if conj:
                y = [ar * br + ai * bi, ai * br - ar * bi]
            else:
                y = [ar * br - ai * bi, ar * bi + ai * br]
            z = mm(three(jnp.concatenate(y, axis=1), 1), inv_three[...])
            out = []
            for c in range(GRP):
                zr = z[c * K1 : (c + 1) * K1, 0:128]
                zi = z[c * K1 : (c + 1) * K1, 128:256]
                out.append(jnp.concatenate([zr * tc - zi * ts, zi * tc + zr * ts], axis=0))
            r = mm(d1_three[...], three(jnp.concatenate(out, axis=1), 0))
            for c in range(GRP):
                dst[pl.ds(grp * GRP + c, BLK, stride=OWN), :] = r[:, c * 128 : (c + 1) * 128]

    forward(sig, spec_h, False)

    def ug_wait(d):
        p = other(d)
        copy(ug_out.at[p], ug_in.at[p], ug_s.at[p], ug_r.at[p], at(p)).wait_recv()

    each(NCTX, ug_wait)
    for s in range(NCTX):
        for h in range(2):
            n = 2 * s + h
            sig_u[n * 16 : (n + 1) * 16, :] = ug_in[s, 0:16, h * 128 : (h + 1) * 128].astype(f32)
            sig[n * 16 : (n + 1) * 16, :] = ug_in[s, 16:32, h * 128 : (h + 1) * 128].astype(f32)
    forward(sig_u, spec_u, True)
    forward(sig, spec_g, True)

    def scatter(result, first_row, out, inn, send, recv):
        for s in range(NCTX):
            x = jnp.concatenate(
                [result[(2 * s + h) * 16 : (2 * s + h + 1) * 16, :] for h in range(2)], axis=1)
            x = x + skip * ug_in[s, first_row : first_row + 16, :].astype(f32)
            out[s] = x.astype(bf16)
        mine = pl.ds(pl.multiple_of(me * 16, 16), 16)
        inn[mine, :] = out[me]

        def go(d):
            p = other(d)
            copy(out.at[p], inn.at[mine, :], send.at[p], recv.at[me], at(p)).start()

        each(NCTX, go)

    backward(spec_u, spec_h, False, sig_u)
    scatter(sig_u, 0, conv_out, conv_in, conv_s, conv_r)
    backward(spec_g, spec_h, True, sig)
    scatter(sig, 16, back_out, back_in, back_s, back_r)

    backward(spec_g, spec_u, True, sig)
    sg_ref[...] = jnp.sum(eye * sig[0:16, 0:1], axis=0, keepdims=True) * scale
    store(7).start()
    for n in range(BLK):
        cols = slice(n * 128, (n + 1) * 128)
        a, b = split(sig[n * 16 : (n + 1) * 16, :] * env[n * 16 : (n + 1) * 16, :])
        bent[0:16, cols] = a
        bent[16:32, cols] = b
        bent[32:48, cols] = a
    total = mm(bent[0:32, :], act[...], 1, 1)
    fog_ref[...] = (total[0:OWN, 0:FH] + total[OWN : 2 * OWN, 0:FH]
                    + pltpu.roll(total[0:OWN, :], FH, 1)[:, 0:FH]) * scale
    store(6).start()

    def slopes(d):
        cols = pl.ds(d * 2 * WIDE, 2 * WIDE)
        a, b = split(mm(w_three, bent[:, cols], 0, 0) * bend[:, cols])
        slope[0:FH, cols] = a
        slope[FH : 2 * FH, cols] = b

    each(SEQ // (2 * WIDE), slopes, 0)
    total = mm(feat[...], slope[...], 1, 1)
    in_sum = (total[0:FEAT, :] + total[FEAT : 2 * FEAT, :] + pltpu.roll(total[0:FEAT, :], FH, 1))
    in_flat[...] = jnp.zeros_like(in_flat)
    in_flat[:, 0:FH] = in_sum[:, 0:FH]
    packed = in_flat[0:24, :] + pltpu.roll(in_flat[24:48, :], 64, 1)
    for k in range(3):
        in_tiles[k] = packed[k * 8 : (k + 1) * 8, :]

    def deal(count, odd, tiles, parts, send, recv, go):
        for k in range(count):
            @pl.when(me != 2 * k + odd)
            def _(k=k):
                c = copy(tiles.at[k], parts.at[me], send.at[k], recv.at[me], at(2 * k + odd))
                go(c)

    deal(3, 1, in_tiles, in_parts, ip_s, ip_r, lambda c: c.start())
    in_owner = jnp.logical_and(lax.rem(me, 2) == 1, me < 6)
    tap_owner = jnp.logical_and(lax.rem(me, 2) == 0, me < 12)
    in_index = jnp.minimum(me // 2, 2)
    tap_index = jnp.minimum(me // 2, 5)

    def rows_wait(out, inn, send, recv):
        def one(d):
            p = other(d)
            rows = pl.ds(pl.multiple_of(p * 16, 16), 16)
            copy(out.at[p], inn.at[rows, :], send.at[p], recv.at[p], at(p)).wait_recv()
        each(NCTX, one)

    rows_wait(conv_out, conv_in, conv_s, conv_r)
    rows_wait(back_out, back_in, back_s, back_r)

    def grad_part(d):
        rows = pl.ds(d * ROWS, ROWS)
        cv = conv_in[rows, :].astype(f32)
        bk = back_in[rows, :].astype(f32)
        mixed_ref[rows, :] = (shorts[0, rows, :] * cv).astype(bf16)
        gs = (cot_ref[rows, :].astype(f32) * cv, bk * shorts[2, rows, :], bk * shorts[1, rows, :])
        for i in range(3):
            grads[i, rows, :] = gs[i]
            hi, lo = split(gs[i][:, 0:128])
            ahead[rows, i * 256 : i * 256 + 128] = hi
            ahead[rows, i * 256 + 128 : i * 256 + 256] = lo

    each(CHUNKS, grad_part, 0)
    store(0).start()
    load(17).wait()
    load(18).wait()
    heads_out[...] = mm(head_sel[...], ahead[...], 1, 1).astype(bf16)
    head_copy = copy(heads_out, heads_in, halo_s.at[1], halo_r.at[1], at(other(NCTX - 1)))
    head_copy.start()

    def collect(parts, tiles, index, recv, sender_count):
        def one(d):
            p = other(d)
            copy(tiles.at[0], parts.at[p], recv.at[p], recv.at[p], at(p)).wait_recv()
        each(NCTX, one)
        parts[me] = tiles[index]
        total = parts[0]
        for p in range(1, sender_count):
            total = total + parts[p]
        return total

    @pl.when(in_owner)
    def _():
        in_quad[member] = collect(in_parts, in_tiles, in_index, ip_r, NCTX)

        def go(d):
            p = quad_peer(d)
            copy(in_quad.at[member], in_quad.at[member], iq_s.at[d], iq_r.at[member],
                 over(p)).start()
        each(quads, go)

    def prod_part(d):
        rows = pl.ds(d * ROWS, ROWS)
        for i in range(3):
            g = grads[i, rows, :]
            for j in range(TAPS):
                x = g * shifted[i * TAPS + j, rows, :].astype(f32)
                hi, lo = split(x[:, 0:128] + x[:, 128:256])
                prods[i * TAPS + j, rows, 0:128] = hi
                prods[i * TAPS + j, rows, 128:256] = lo

    each(CHUNKS, prod_part, 0)
    pick_row = lax.broadcasted_iota(jnp.int32, (32, 256), 0)
    total = jnp.zeros((32, 256), f32)
    for i in range(3):
        for j in range(TAPS):
            pick = (pick_row == i * 8 + j).astype(f32).astype(bf16)
            total = total + mm(pick, prods[i * TAPS + j], 1, 1)
    for k in range(6):
        tap_tiles[k] = total[(k // 2) * 8 : (k // 2) * 8 + 8, (k % 2) * 128 : (k % 2) * 128 + 128]
    deal(6, 0, tap_tiles, tap_parts, tp_s, tp_r, lambda c: c.start())

    @pl.when(in_owner)
    def _():
        def one(d):
            p = lax.rem(member + d, quads)
            copy(in_quad.at[p], in_quad.at[p], iq_s.at[d], iq_r.at[p], over(quad_peer(d))).wait_recv()
        each(quads, one)
        t = in_quad[0]
        for p in range(1, quads):
            t = t + in_quad[p]
        in_stack[layer] = t

        def go(d):
            copy(in_stack.at[layer], in_stack.at[layer], iz_s.at[d], iz_r.at[layer],
                 over(stack_peer(d))).start()
        each(stacks, go)

    head_copy.wait_recv()
    before_end = jnp.where(me < NCTX - 1, 1.0, 0.0)
    after[...] = mm(heads_in[...], head_place[...], 0, 0) * before_end
    lane = lax.broadcasted_iota(jnp.int32, (ROWS, 128), 1)

    def proj(i, ref):
        def proj_part(d):
            rows = slice(d * ROWS, (d + 1) * ROWS)
            left, right = grads[i, rows, 0:128], grads[i, rows, 128:256]
            tap = tap_wide[i * TAPS, rows, :]
            acc = [tap * left, tap * right]
            for j in range(1, TAPS):
                tap = tap_wide[i * TAPS + j, rows, :]
                near, far = pltpu.roll(left, 128 - j, 1), pltpu.roll(right, 128 - j, 1)
                edge = after[rows, (i * 6 + j - 1) * 128 : (i * 6 + j) * 128]
                here = lane < 128 - j
                acc[0] = acc[0] + tap * jnp.where(here, near, far)
                acc[1] = acc[1] + tap * jnp.where(here, far, edge)
            ref[rows, 0:128] = acc[0].astype(bf16)
            ref[rows, 128:256] = acc[1].astype(bf16)

        for d in range(CHUNKS):
            proj_part(d)
        store(1 + i).start()

    proj(0, qg_ref)

    @pl.when(tap_owner)
    def _():
        tap_sums[tap_index] = collect(tap_parts, tap_tiles, tap_index, tp_r, NCTX)

        def go(d):
            copy(tap_sums.at[tap_index], tap_sums.at[tap_index], ts_s.at[d], ts_r.at[tap_index],
                 at(other(d))).start()
        each(NCTX, go)

    @pl.when(in_owner)
    def _():
        def one(d):
            p = lax.rem(layer + d, stacks)
            copy(in_stack.at[p], in_stack.at[p], iz_s.at[d], iz_r.at[p], over(stack_peer(d))).wait_recv()
        each(stacks, one)
        t = in_stack[0]
        for p in range(1, stacks):
            t = t + in_stack[p]
        in_sums[in_index] = t

        def go(d):
            copy(in_sums.at[in_index], in_sums.at[in_index], is_s.at[d], is_r.at[in_index],
                 at(other(d))).start()
        each(NCTX, go)

    proj(1, kg_ref)
    proj(2, vg_ref)

    for k in range(6):
        @pl.when(me != 2 * k)
        def _(k=k):
            copy(tap_sums.at[k], tap_sums.at[k], ts_s.at[0], ts_r.at[k], at(2 * k)).wait_recv()
    for i in range(3):
        both = jnp.concatenate([tap_sums[2 * i], tap_sums[2 * i + 1]], axis=1) * scale
        tg_ref[i] = both[0:TAPS, :]
    store(4).start()
    for k in range(3):
        @pl.when(me != 2 * k + 1)
        def _(k=k):
            copy(in_sums.at[k], in_sums.at[k], is_s.at[0], is_r.at[k], at(2 * k + 1)).wait_recv()
    sums = jnp.concatenate([in_sums[k] for k in range(3)], axis=0) * (scale / math.sqrt(D))
    fig_ref[0:24, :] = sums[:, 0:FH]
    fig_ref[24:EMB, :] = pltpu.roll(sums, 64, 1)[0 : EMB - 24, 0:FH]
    store(5).start()

    for k in range(8):
        store(k).wait()
    tail_copy.wait_send()
    head_copy.wait_send()
    deal(3, 1, in_tiles, in_parts, ip_s, ip_r, lambda c: c.wait_send())
    deal(6, 0, tap_tiles, tap_parts, tp_s, tp_r, lambda c: c.wait_send())

    def left(d):
        p = other(d)
        mine = pl.ds(pl.multiple_of(me * 16, 16), 16)
        copy(ug_out.at[p], ug_in.at[me], ug_s.at[p], ug_r.at[me], at(p)).wait_send()
        copy(conv_out.at[p], conv_in.at[mine, :], conv_s.at[p], conv_r.at[me], at(p)).wait_send()
        copy(back_out.at[p], back_in.at[mine, :], back_s.at[p], back_r.at[me], at(p)).wait_send()

    each(NCTX, left)

    @pl.when(in_owner)
    def _():
        each(quads, lambda d: copy(in_quad.at[member], in_quad.at[member], iq_s.at[d],
                                   iq_r.at[member], over(quad_peer(d))).wait_send())
        each(stacks, lambda d: copy(in_stack.at[layer], in_stack.at[layer], iz_s.at[d],
                                    iz_r.at[layer], over(stack_peer(d))).wait_send())
        each(NCTX, lambda d: copy(in_sums.at[in_index], in_sums.at[in_index], is_s.at[d],
                                  is_r.at[in_index], at(other(d))).wait_send())

    @pl.when(tap_owner)
    def _():
        each(NCTX, lambda d: copy(tap_sums.at[tap_index], tap_sums.at[tap_index], ts_s.at[d],
                                  ts_r.at[tap_index], at(other(d))).wait_send())


def hand_on(*refs):
    held, load_s, store_s = refs[16:24], refs[24], refs[25]
    loads = [pltpu.make_async_copy(refs[k], held[k], load_s.at[k]) for k in range(8)]
    stores = [pltpu.make_async_copy(held[k], refs[8 + k], store_s.at[k]) for k in range(8)]
    for c in loads:
        c.start()
    for k in range(8):
        loads[k].wait()
        stores[k].start()
    for c in stores:
        c.wait()


def per_device(consts, chans, query_proj, key_proj, value_proj, out_cotangent, short_taps,
               filter_in, filter_out, decay_rate, skip_gain):
    quads = math.gcd(chans, 4)
    stacks = chans // quads
    block = jax.ShapeDtypeStruct((256, POS), bf16)
    dma = pltpu.SemaphoreType.DMA
    V = pltpu.VMEM
    args = [query_proj, key_proj, value_proj, out_cotangent, short_taps, filter_in, filter_out.T,
            decay_rate.reshape(1, OWN), skip_gain.reshape(1, OWN)]
    args += [jnp.asarray(c) for c in consts]
    shapes = (block, block, block, block,
              jax.ShapeDtypeStruct((3, TAPS, 256), f32),
              jax.ShapeDtypeStruct((EMB, FH), f32),
              jax.ShapeDtypeStruct((OWN, FH), f32),
              jax.ShapeDtypeStruct((1, OWN), f32))
    hbm = pl.BlockSpec(memory_space=pl.ANY)
    outs = pl.pallas_call(
        functools.partial(kernel, quads, stacks),
        out_shape=shapes,
        in_specs=[hbm] * LOADS,
        out_specs=[hbm] * 8,
        scratch_shapes=[V(a.shape, a.dtype) for a in args] + [V(a.shape, a.dtype) for a in shapes] + [
            dma((LOADS,)), dma((8,)),
            V((32, 256), bf16), V((32, 256), bf16), V((48, 256), bf16), V((48, 256), bf16),
            V((24, 256), f32), V((256, 128), f32), V((FEAT, FH), f32),
            V((21, 256, 128), f32), V((256, 384), bf16), V((256, 18 * 128), f32),
            V((3, 256, 256), f32), V((21, 256, 256), bf16),
            V((3, 256, 256), f32), V((256, 768), bf16), V((FH, SEQ), f32),
            V((2 * FH, SEQ), bf16), V((512, 128), f32),
            V((512, 128), f32), V((512, 128), f32),
            V((OWN * K1, 256), f32), V((OWN * K1, 256), f32), V((OWN * K1, 256), f32),
            V((NCTX, 32, 256), bf16), V((NCTX, 32, 256), bf16),
            V((NCTX, 16, 256), bf16), V((256, 256), bf16),
            V((NCTX, 16, 256), bf16), V((256, 256), bf16),
            V((3 * OWN, SEQ), bf16), V((2 * FH, SEQ), bf16),
            V((21, 256, 256), bf16), V((6, 8, 128), f32), V((NCTX, 8, 128), f32),
            V((6, 8, 128), f32),
            V((3, 8, 128), f32), V((NCTX, 8, 128), f32),
            V((quads, 8, 128), f32), V((stacks, 8, 128), f32),
            V((3, 8, 128), f32), V((48, 128), f32),
            dma((2,)), dma((2,)), dma((NCTX,)), dma((NCTX,)),
            dma((NCTX,)), dma((NCTX,)), dma((NCTX,)), dma((NCTX,)),
            dma((6,)), dma((NCTX,)), dma((NCTX,)), dma((6,)),
            dma((3,)), dma((NCTX,)), dma((quads,)), dma((quads,)),
            dma((stacks,)), dma((stacks,)), dma((NCTX,)), dma((3,)),
        ],
        compiler_params=pltpu.CompilerParams(
            collective_id=0, has_side_effects=True, vmem_limit_bytes=56 * 1024 * 1024),
    )(*args)
    outs = pl.pallas_call(
        hand_on,
        out_shape=shapes,
        in_specs=[hbm] * 8,
        out_specs=[hbm] * 8,
        scratch_shapes=[V(a.shape, a.dtype) for a in shapes] + [dma((8,)), dma((8,))],
    )(*outs)
    return outs[:6] + (outs[6].T, outs[7].reshape(OWN))


def solution(mesh):
    consts = tables()
    return jax.shard_map(
        functools.partial(per_device, consts, mesh.shape["chan"]),
        mesh=mesh,
        in_specs=(
            P("chan", "ctx"),
            P("chan", "ctx"),
            P("chan", "ctx"),
            P("chan", "ctx"),
            P(None, None, "chan"),
            P(),
            P(None, ("chan", "ctx")),
            P(("chan", "ctx")),
            P(("chan", "ctx")),
        ),
        out_specs=(
            P("chan", "ctx"),
            P("chan", "ctx"),
            P("chan", "ctx"),
            P("chan", "ctx"),
            P(None, None, "chan"),
            P(),
            P(None, ("chan", "ctx")),
            P(("chan", "ctx")),
        ),
        check_vma=False,
    )
```

```python
import functools
import math

import jax
import jax.numpy as jnp
import ml_dtypes
import numpy as np
from jax import lax
from jax.experimental import pallas as pl
from jax.experimental.pallas import tpu as pltpu
from jax.sharding import PartitionSpec as P

D = 8192
SEQ = 4096
EMB = 33
FH = 64
TAPS = 7
NCTX = 16
POS = SEQ // NCTX
OWN = 16
K1 = 40
N1 = 64
N2 = 128
BLK = SEQ // N2
FEAT = 48
LOADS = 19
YS = 8
STEPS = sorted(((dx, dy) for dx in range(2) for dy in range(YS) if dx + dy > 0),
               key=lambda s: (-s[0] - min(s[1], YS - s[1]), s))
MESH = pl.DeviceIdType.MESH
f32 = jnp.float32
bf16 = jnp.bfloat16


def halves(x):
    x = np.asarray(x, np.float32)
    hi = x.astype(ml_dtypes.bfloat16)
    lo = (x - hi.astype(np.float32)).astype(ml_dtypes.bfloat16)
    return hi, lo


def tables():
    k1 = np.arange(K1)[:, None]
    live = (k1 <= N1 // 2).astype(np.float64)
    n = np.arange(BLK)[None, :]
    ang = 2 * np.pi * ((k1 * n) % N1) / N1
    c1 = np.concatenate([np.cos(ang) * live, -np.sin(ang) * live], 0)
    hi, lo = halves(c1)
    c1_two = np.concatenate([hi, lo], 1)
    c1_three = np.concatenate([hi, hi, lo], 1)
    weight = np.where((k1 == 0) | (k1 == N1 // 2), 1.0, 2.0) * live / (N1 * N2)
    d1 = np.concatenate([np.cos(ang) * weight, -np.sin(ang) * weight], 0).T
    hi, lo = halves(d1)
    d1_three = np.concatenate([hi, hi, lo], 1)
    m = np.arange(N2)
    turn = 2 * np.pi * ((m[:, None] * m[None, :]) % N2) / N2
    c, s = np.cos(turn), np.sin(turn)
    fwd = np.block([[c, -s], [s, c]])
    hi, lo = halves(fwd)
    fwd_three = np.concatenate([hi, hi, lo], 0)
    hi, lo = halves(fwd.T)
    inv_three = np.concatenate([hi, hi, lo], 0)
    twist = 2 * np.pi * ((k1 * m[None, :]) % (N1 * N2)) / (N1 * N2)
    twist = np.concatenate([np.cos(twist), np.sin(twist)], 0).astype(np.float32)
    t = np.arange(SEQ)
    bands = (EMB - 1) // 2
    b = np.arange(1, bands + 1)
    phase = 2 * np.pi * ((b[:, None] * t[None, :]) % SEQ) / SEQ
    feat = np.zeros((FEAT, SEQ))
    feat[0] = t / SEQ
    feat[1 : 1 + bands] = np.cos(phase)
    feat[1 + bands : 1 + 2 * bands] = np.sin(phase)
    feat_two = np.concatenate(halves(feat), 0)
    tail = np.zeros((32, 3 * 128), np.float32)
    head = np.zeros((48, 6 * 128), np.float32)
    place = np.zeros((48, 18 * 128), np.float32)
    for i in range(3):
        for r in range(8):
            tail[i * 8 + r, i * 128 + 120 + r] = 1
            for h in range(2):
                head[i * 16 + h * 8 + r, (i * 2 + h) * 128 + r] = 1
                for j in range(r + 1, TAPS):
                    place[i * 16 + h * 8 + r, (i * 6 + j - 1) * 128 + 128 + r - j] = 1
    as16 = lambda x: x.astype(ml_dtypes.bfloat16)
    return (c1_two, c1_three, d1_three, fwd_three, inv_three, twist, feat_two,
            as16(tail), as16(head), as16(place))


def split(x):
    hi = x.astype(bf16)
    return hi, (x - hi.astype(f32)).astype(bf16)


def mm(a, b, ca=1, cb=0):
    return lax.dot_general(a, b, (((ca,), (cb,)), ((), ())), preferred_element_type=f32)


def sin_cos(x):
    n = jnp.floor(x * (1.0 / math.pi) + 0.5)
    r = x - n * 3.140625
    r = r - n * 9.67502593994140625e-4
    r = r - n * 1.509957990978376e-7
    sign = 1.0 - 2.0 * (n - 2.0 * jnp.floor(n * 0.5))
    z = r * r
    s = -1.0 / 39916800.0
    for k in (1.0 / 362880.0, -1.0 / 5040.0, 1.0 / 120.0, -1.0 / 6.0, 1.0):
        s = s * z + k
    c = 1.0 / 479001600.0
    for k in (-1.0 / 3628800.0, 1.0 / 40320.0, -1.0 / 720.0, 1.0 / 24.0, -0.5, 1.0):
        c = c * z + k
    return s * r * sign, c * sign


def kernel(chans,
           *refs):
    sources, refs = refs[:LOADS], refs[LOADS:]
    targets, refs = refs[:8], refs[8:]
    held, refs = refs[:LOADS], refs[LOADS:]
    done, refs = refs[:8], refs[8:]
    (q_ref, k_ref, v_ref, cot_ref, taps_ref, fin_ref, fout_ref, decay_ref, skip_ref,
     c1_two, c1_three, d1_three, fwd_three, inv_three, twist, feat,
     tail_sel, head_sel, head_place) = held
    mixed_ref, qg_ref, kg_ref, vg_ref, tg_ref, fig_ref, fog_ref, sg_ref = done
    (load_s, store_s, tails_out, tails_in, heads_out, heads_in, tap_rows, tap_cols, fin_pad,
     tap_wide, prev, after, shorts, shifted, grads, ahead, bend, act, env,
     sig, sig_u, spec_h, spec_u, spec_g,
     u_out, u_in, g_out, g_in, conv_out, conv_in, back_out, back_in, bent, slope,
     prods, tap_out, tap_in, in_tiles, in_parts, in_row, in_sums, in_flat,
     halo_s, halo_r, u_s, u_r, g_s, g_r, conv_s, conv_r, back_s, back_r,
     tp_s, tp_r, ip_s, ip_r, iq_s, iq_r, is_s, is_r) = refs
    me = lax.axis_index("ctx")
    ch = lax.axis_index("chan")

    def at(ctx_index):
        return {"ctx": ctx_index, "chan": ch}

    def over(chan_index):
        return {"ctx": me, "chan": chan_index}

    def copy(src, dst, send, recv, where):
        return pltpu.make_async_remote_copy(
            src_ref=src, dst_ref=dst, send_sem=send, recv_sem=recv,
            device_id=where, device_id_type=MESH)

    def each(count, body, start=1):
        for d in range(start, count):
            body(d)

    def other(d):
        return lax.rem(me + d, NCTX)

    def peers(body):
        for dx, dy in STEPS:
            body(lax.rem(me // YS + dx, NCTX // YS) * YS + lax.rem(me % YS + dy, YS))

    def chan_peer(d):
        return lax.rem(ch + d, chans)

    in_owner = jnp.logical_and(lax.rem(me, 2) == 1, me < 6)
    in_index = jnp.minimum(me // 2, 2)

    barrier = pltpu.get_barrier_semaphore()

    def greet(where):
        pl.semaphore_signal(barrier, inc=1, device_id=where, device_id_type=MESH)

    peers(lambda p: greet(at(p)))

    @pl.when(in_owner)
    def _():
        each(chans, lambda d: greet(over(chan_peer(d))))

    def load(k):
        return pltpu.make_async_copy(sources[k], held[k], load_s.at[k])

    def store(k):
        return pltpu.make_async_copy(done[k], targets[k], store_s.at[k])

    for k in (0, 1, 2, 16, 4, 5, 15, 3, 6, 7, 8, 14, 10, 12, 9, 11, 13, 17, 18):
        load(k).start()

    for k in (0, 1, 2, 16):
        load(k).wait()
    ends = jnp.concatenate([r[:, 128:256] for r in (q_ref, k_ref, v_ref)], axis=1)
    tails_out[...] = mm(tail_sel[...], ends, 1, 1).astype(bf16)
    pl.semaphore_wait(barrier, jnp.where(in_owner, NCTX - 1 + chans - 1, NCTX - 1))
    tail_copy = copy(tails_out, tails_in, halo_s.at[0], halo_r.at[0], at(other(1)))
    tail_copy.start()

    load(4).wait()
    tap_rows[...] = jnp.zeros_like(tap_rows)
    for i in range(3):
        tap_rows[i * 8 : i * 8 + TAPS, :] = taps_ref[i]
    row = lax.broadcasted_iota(jnp.int32, (24, 128), 0)
    col = lax.broadcasted_iota(jnp.int32, (24, 128), 1)
    unit = (row == col).astype(bf16)
    hi, lo = split(tap_rows[...])
    rest = (tap_rows[...] - hi.astype(f32) - lo.astype(f32)).astype(bf16)
    tap_cols[...] = mm(hi, unit, 0, 0) + mm(lo, unit, 0, 0) + mm(rest, unit, 0, 0)
    ROWS = 32
    CHUNKS = 256 // ROWS

    def spread(d):
        rows = pl.ds(d * ROWS, ROWS)
        for i in range(3):
            for j in range(TAPS):
                one = tap_cols[rows, i * 8 + j : i * 8 + j + 1]
                tap_wide[i * TAPS + j, rows, :] = jnp.broadcast_to(one, (ROWS, 128))

    each(CHUNKS, spread, 0)

    load(5).wait()
    load(15).wait()
    fin_pad[...] = jnp.zeros_like(fin_pad)
    fin_pad[0:EMB, :] = fin_ref[...]
    fin_hi, fin_lo = split(fin_pad[...])
    fin_three = jnp.concatenate([fin_hi, fin_hi, fin_lo], axis=0)
    WIDE = 512

    def network(d):
        cols = pl.ds(d * WIDE, WIDE)
        f = feat[:, cols]
        pre = mm(fin_three, jnp.concatenate([f, f[0:FEAT, :]], axis=0), 0, 0)
        s, c = sin_cos(pre)
        bend[:, cols] = c
        a, b = split(s)
        act[0:FH, cols] = a
        act[FH : 2 * FH, cols] = b

    each(SEQ // WIDE, network, 0)

    tail_copy.wait_recv()
    inside = jnp.where(me > 0, 1.0, 0.0)
    prev[...] = (mm(tails_in[...], tail_sel[...], 0, 0) * inside).astype(bf16)

    def moved(x, by):
        return x if by == 0 else pltpu.roll(x, by, 1)

    def short(i, ref, rows):
        x = jnp.concatenate([prev[rows, i * 128 : (i + 1) * 128], ref[rows, :]], axis=1)
        acc = None
        for j in range(TAPS):
            y = moved(x, j)[:, 128:384]
            shifted[i * TAPS + j, rows, :] = y
            tap = tap_wide[i * TAPS + j, rows, :]
            term = jnp.concatenate([tap, tap], axis=1) * y.astype(f32)
            acc = term if acc is None else acc + term
        shorts[i, rows, :] = acc
        return acc

    def scatter(out, inn, send, recv):
        inn[me] = out[me]
        peers(lambda p: copy(out.at[p], inn.at[me], send.at[p], recv.at[me], at(p)).start())

    def short_part(which, out):
        for part in range(CHUNKS):
            rows = pl.ds(part * ROWS, ROWS)
            if which == 0:
                x = short(1, k_ref, rows) * short(2, v_ref, rows)
            else:
                x = cot_ref[rows, :].astype(f32) * short(0, q_ref, rows)
            for h in range(2):
                out[part * 2 + h] = x[h * 16 : (h + 1) * 16, :].astype(bf16)

    short_part(0, u_out)
    scatter(u_out, u_in, u_s, u_r)
    load(3).wait()
    short_part(1, g_out)
    scatter(g_out, g_in, g_s, g_r)

    for k in (6, 7, 8):
        load(k).wait()
    eye = (lax.broadcasted_iota(jnp.int32, (OWN, OWN), 0)
           == lax.broadcasted_iota(jnp.int32, (OWN, OWN), 1)).astype(f32)
    decay = jnp.sum(eye * decay_ref[...], axis=1, keepdims=True)
    skip = jnp.sum(eye * skip_ref[...], axis=1, keepdims=True)
    w_hi, w_lo = split(fout_ref[...])
    w_two = jnp.concatenate([w_hi, w_lo], axis=0)
    w_three = jnp.concatenate([w_hi, w_hi, w_lo], axis=0)
    scale = 1.0 / math.sqrt(SEQ)

    def filters(d):
        cols = pl.ds(d * WIDE, WIDE)
        raw = mm(w_two, act[0:FH, cols])
        raw = raw[0:OWN, :] + raw[OWN : 2 * OWN, :] + mm(w_hi, act[FH : 2 * FH, cols])
        t = (d * WIDE + lax.broadcasted_iota(jnp.int32, (OWN, WIDE), 1)).astype(f32)
        e = jnp.exp(-decay * (t * (1.0 / SEQ))) * scale
        h = raw * e
        for n in range(WIDE // 128):
            rows = pl.ds((d * (WIDE // 128) + n) * OWN, OWN)
            env[rows, :] = e[:, n * 128 : (n + 1) * 128]
            sig[rows, :] = h[:, n * 128 : (n + 1) * 128]

    each(SEQ // WIDE, filters, 0)

    for k in (9, 10, 11, 12, 13, 14):
        load(k).wait()
    GRP = 4
    tc, ts = twist[0:K1, :], twist[K1 : 2 * K1, :]

    def three(x, axis):
        hi, lo = split(x)
        return jnp.concatenate([hi, lo, hi], axis=axis)

    def forward(src, spec, exact):
        for grp in range(OWN // GRP):
            x = jnp.concatenate(
                [src[pl.ds(grp * GRP + c, BLK, stride=OWN), :] for c in range(GRP)], axis=1)
            if exact:
                x = x.astype(bf16)
                a = mm(c1_two[...], jnp.concatenate([x, x], axis=0))
            else:
                a = mm(c1_three[...], three(x, 0))
            re, im = [], []
            for c in range(GRP):
                ar = a[0:K1, c * 128 : (c + 1) * 128]
                ai = a[K1 : 2 * K1, c * 128 : (c + 1) * 128]
                re.append(ar * tc + ai * ts)
                im.append(ai * tc - ar * ts)
            x = jnp.concatenate([jnp.concatenate(re, 0), jnp.concatenate(im, 0)], axis=1)
            spec[grp * GRP * K1 : (grp + 1) * GRP * K1, :] = mm(three(x, 1), fwd_three[...])

    def backward(first, second, conj, dst):
        for grp in range(OWN // GRP):
            rows = slice(grp * GRP * K1, (grp + 1) * GRP * K1)
            ar, ai = first[rows, 0:128], first[rows, 128:256]
            br, bi = second[rows, 0:128], second[rows, 128:256]
            if conj:
                y = [ar * br + ai * bi, ai * br - ar * bi]
            else:
                y = [ar * br - ai * bi, ar * bi + ai * br]
            z = mm(three(jnp.concatenate(y, axis=1), 1), inv_three[...])
            out = []
            for c in range(GRP):
                zr = z[c * K1 : (c + 1) * K1, 0:128]
                zi = z[c * K1 : (c + 1) * K1, 128:256]
                out.append(jnp.concatenate([zr * tc - zi * ts, zi * tc + zr * ts], axis=0))
            r = mm(d1_three[...], three(jnp.concatenate(out, axis=1), 0))
            for c in range(GRP):
                dst[pl.ds(grp * GRP + c, BLK, stride=OWN), :] = r[:, c * 128 : (c + 1) * 128]

    forward(sig, spec_h, False)

    def wait_all(out, inn, send, recv):
        peers(lambda p: copy(out.at[p], inn.at[p], send.at[p], recv.at[p], at(p)).wait_recv())

    def unfold(inn, dst):
        for n in range(BLK):
            half = n % 2 * 128
            dst[n * 16 : (n + 1) * 16, :] = inn[n // 2, :, half : half + 128].astype(f32)

    def fold(result, direct, out):
        for s in range(NCTX):
            x = jnp.concatenate(
                [result[(2 * s + h) * 16 : (2 * s + h + 1) * 16, :] for h in range(2)], axis=1)
            out[s] = (x + skip * direct[s].astype(f32)).astype(bf16)

    wait_all(u_out, u_in, u_s, u_r)
    unfold(u_in, sig_u)
    forward(sig_u, spec_u, True)
    backward(spec_u, spec_h, False, sig_u)
    fold(sig_u, u_in, conv_out)
    scatter(conv_out, conv_in, conv_s, conv_r)
    wait_all(g_out, g_in, g_s, g_r)
    unfold(g_in, sig)
    forward(sig, spec_g, True)

    backward(spec_g, spec_u, True, sig)
    sg_ref[...] = jnp.sum(eye * sig[0:16, 0:1], axis=0, keepdims=True) * scale
    store(7).start()
    for n in range(BLK):
        cols = slice(n * 128, (n + 1) * 128)
        a, b = split(sig[n * 16 : (n + 1) * 16, :] * env[n * 16 : (n + 1) * 16, :])
        bent[0:16, cols] = a
        bent[16:32, cols] = b
        bent[32:48, cols] = a
    def slopes(d):
        cols = pl.ds(d * 2 * WIDE, 2 * WIDE)
        a, b = split(mm(w_three, bent[:, cols], 0, 0) * bend[:, cols])
        slope[0:FH, cols] = a
        slope[FH : 2 * FH, cols] = b

    each(SEQ // (2 * WIDE), slopes, 0)
    total = mm(feat[...], slope[...], 1, 1)
    in_sum = (total[0:FEAT, :] + total[FEAT : 2 * FEAT, :] + pltpu.roll(total[0:FEAT, :], FH, 1))
    in_flat[...] = jnp.zeros_like(in_flat)
    in_flat[:, 0:FH] = in_sum[:, 0:FH]
    packed = in_flat[0:24, :] + pltpu.roll(in_flat[24:48, :], 64, 1)
    for k in range(3):
        in_tiles[k] = packed[k * 8 : (k + 1) * 8, :]

    def deal(go):
        for k in range(3):
            @pl.when(me != 2 * k + 1)
            def _(k=k):
                go(copy(in_tiles.at[k], in_parts.at[me], ip_s.at[k], ip_r.at[me], at(2 * k + 1)))

    deal(lambda c: c.start())
    backward(spec_g, spec_h, True, sig)
    fold(sig, g_in, back_out)
    scatter(back_out, back_in, back_s, back_r)
    total = mm(bent[0:32, :], act[...], 1, 1)
    fog_ref[...] = (total[0:OWN, 0:FH] + total[OWN : 2 * OWN, 0:FH]
                    + pltpu.roll(total[0:OWN, :], FH, 1)[:, 0:FH]) * scale
    store(6).start()

    def take(i, g, rows):
        grads[i, rows, :] = g
        hi, lo = split(g[:, 0:128])
        ahead[rows, i * 256 : i * 256 + 128] = hi
        ahead[rows, i * 256 + 128 : i * 256 + 256] = lo
        for j in range(TAPS):
            x = g * shifted[i * TAPS + j, rows, :].astype(f32)
            hi, lo = split(x[:, 0:128] + x[:, 128:256])
            prods[i * TAPS + j, rows, 0:128] = hi
            prods[i * TAPS + j, rows, 128:256] = lo

    pick_row = lax.broadcasted_iota(jnp.int32, (16, 256), 0)

    def tap_sum(k, which):
        total = jnp.zeros((16, 256), f32)
        for n, i in enumerate(which):
            for j in range(TAPS):
                pick = (pick_row == n * 8 + j).astype(f32).astype(bf16)
                total = total + mm(pick, prods[i * TAPS + j], 1, 1)
        tap_out[k] = total.astype(bf16)
        tap_in[k, me] = tap_out[k]
        peers(lambda p: copy(tap_out.at[k], tap_in.at[k, me], tp_s.at[k, p], tp_r.at[k, me],
                             at(p)).start())

    def conv_part(d):
        rows = pl.ds(d * ROWS, ROWS)
        cv = jnp.concatenate([conv_in[2 * d], conv_in[2 * d + 1]], axis=0).astype(f32)
        mixed_ref[rows, :] = (shorts[0, rows, :] * cv).astype(bf16)
        take(0, cot_ref[rows, :].astype(f32) * cv, rows)

    def back_part(d):
        rows = pl.ds(d * ROWS, ROWS)
        bk = jnp.concatenate([back_in[2 * d], back_in[2 * d + 1]], axis=0).astype(f32)
        take(1, bk * shorts[2, rows, :], rows)
        take(2, bk * shorts[1, rows, :], rows)

    wait_all(conv_out, conv_in, conv_s, conv_r)
    each(CHUNKS, conv_part, 0)
    store(0).start()
    tap_sum(0, (0,))

    @pl.when(in_owner)
    def _():
        peers(lambda p: copy(in_tiles.at[0], in_parts.at[p], ip_r.at[p], ip_r.at[p],
                             at(p)).wait_recv())
        in_parts[me] = in_tiles[in_index]
        t = in_parts[0]
        for p in range(1, NCTX):
            t = t + in_parts[p]
        in_row[ch] = t
        each(chans, lambda d: copy(in_row.at[ch], in_row.at[ch], iq_s.at[d], iq_r.at[ch],
                                   over(chan_peer(d))).start())

    load(17).wait()
    load(18).wait()
    wait_all(back_out, back_in, back_s, back_r)
    each(CHUNKS, back_part, 0)
    heads_out[...] = mm(head_sel[...], ahead[...], 1, 1).astype(bf16)
    head_copy = copy(heads_out, heads_in, halo_s.at[1], halo_r.at[1], at(other(NCTX - 1)))
    head_copy.start()
    tap_sum(1, (1, 2))

    head_copy.wait_recv()
    before_end = jnp.where(me < NCTX - 1, 1.0, 0.0)
    after[...] = mm(heads_in[...], head_place[...], 0, 0) * before_end
    lane = lax.broadcasted_iota(jnp.int32, (ROWS, 128), 1)

    def proj(i, ref):
        def proj_part(d):
            rows = slice(d * ROWS, (d + 1) * ROWS)
            left, right = grads[i, rows, 0:128], grads[i, rows, 128:256]
            tap = tap_wide[i * TAPS, rows, :]
            acc = [tap * left, tap * right]
            for j in range(1, TAPS):
                tap = tap_wide[i * TAPS + j, rows, :]
                near, far = pltpu.roll(left, 128 - j, 1), pltpu.roll(right, 128 - j, 1)
                edge = after[rows, (i * 6 + j - 1) * 128 : (i * 6 + j) * 128]
                here = lane < 128 - j
                acc[0] = acc[0] + tap * jnp.where(here, near, far)
                acc[1] = acc[1] + tap * jnp.where(here, far, edge)
            ref[rows, 0:128] = acc[0].astype(bf16)
            ref[rows, 128:256] = acc[1].astype(bf16)

        for d in range(CHUNKS):
            proj_part(d)
        store(1 + i).start()

    proj(0, qg_ref)
    proj(1, kg_ref)
    proj(2, vg_ref)

    @pl.when(in_owner)
    def _():
        def one(d):
            p = chan_peer(d)
            copy(in_row.at[p], in_row.at[p], iq_s.at[d], iq_r.at[p], over(p)).wait_recv()
        each(chans, one)
        t = in_row[0]
        for p in range(1, chans):
            t = t + in_row[p]
        in_sums[in_index] = t
        peers(lambda p: copy(in_sums.at[in_index], in_sums.at[in_index], is_s.at[p],
                             is_r.at[in_index], at(p)).start())

    for k in range(2):
        peers(lambda p: copy(tap_out.at[k], tap_in.at[k, p], tp_s.at[k, p], tp_r.at[k, p],
                             at(p)).wait_recv())
        t = tap_in[k, 0].astype(f32)
        for p in range(1, NCTX):
            t = t + tap_in[k, p].astype(f32)
        if k == 0:
            tg_ref[0] = t[0:TAPS, :] * scale
        else:
            tg_ref[1] = t[0:TAPS, :] * scale
            tg_ref[2] = t[8 : 8 + TAPS, :] * scale
    store(4).start()
    for k in range(3):
        @pl.when(me != 2 * k + 1)
        def _(k=k):
            copy(in_sums.at[k], in_sums.at[k], is_s.at[0], is_r.at[k], at(2 * k + 1)).wait_recv()
    sums = jnp.concatenate([in_sums[k] for k in range(3)], axis=0) * (scale / math.sqrt(D))
    fig_ref[0:24, :] = sums[:, 0:FH]
    fig_ref[24:EMB, :] = pltpu.roll(sums, 64, 1)[0 : EMB - 24, 0:FH]
    store(5).start()

    for k in range(8):
        store(k).wait()
    tail_copy.wait_send()
    head_copy.wait_send()
    deal(lambda c: c.wait_send())

    def left(p):
        for out, inn, send, recv in ((u_out, u_in, u_s, u_r), (g_out, g_in, g_s, g_r),
                                     (conv_out, conv_in, conv_s, conv_r),
                                     (back_out, back_in, back_s, back_r)):
            copy(out.at[p], inn.at[me], send.at[p], recv.at[me], at(p)).wait_send()
        for k in range(2):
            copy(tap_out.at[k], tap_in.at[k, me], tp_s.at[k, p], tp_r.at[k, me], at(p)).wait_send()

    peers(left)

    @pl.when(in_owner)
    def _():
        each(chans, lambda d: copy(in_row.at[ch], in_row.at[ch], iq_s.at[d], iq_r.at[ch],
                                   over(chan_peer(d))).wait_send())
        peers(lambda p: copy(in_sums.at[in_index], in_sums.at[in_index], is_s.at[p],
                             is_r.at[in_index], at(p)).wait_send())


def hand_on(*refs):
    held, load_s, store_s = refs[16:24], refs[24], refs[25]
    loads = [pltpu.make_async_copy(refs[k], held[k], load_s.at[k]) for k in range(8)]
    stores = [pltpu.make_async_copy(held[k], refs[8 + k], store_s.at[k]) for k in range(8)]
    for c in loads:
        c.start()
    for k in range(8):
        loads[k].wait()
        stores[k].start()
    for c in stores:
        c.wait()


def per_device(consts, chans, query_proj, key_proj, value_proj, out_cotangent, short_taps,
               filter_in, filter_out, decay_rate, skip_gain):
    block = jax.ShapeDtypeStruct((256, POS), bf16)
    dma = pltpu.SemaphoreType.DMA
    V = pltpu.VMEM
    args = [query_proj, key_proj, value_proj, out_cotangent, short_taps, filter_in, filter_out.T,
            decay_rate.reshape(1, OWN), skip_gain.reshape(1, OWN)]
    args += [jnp.asarray(c) for c in consts]
    shapes = (block, block, block, block,
              jax.ShapeDtypeStruct((3, TAPS, 256), f32),
              jax.ShapeDtypeStruct((EMB, FH), f32),
              jax.ShapeDtypeStruct((OWN, FH), f32),
              jax.ShapeDtypeStruct((1, OWN), f32))
    hbm = pl.BlockSpec(memory_space=pl.ANY)
    outs = pl.pallas_call(
        functools.partial(kernel, chans),
        out_shape=shapes,
        in_specs=[hbm] * LOADS,
        out_specs=[hbm] * 8,
        scratch_shapes=[V(a.shape, a.dtype) for a in args] + [V(a.shape, a.dtype) for a in shapes] + [
            dma((LOADS,)), dma((8,)),
            V((32, 256), bf16), V((32, 256), bf16), V((48, 256), bf16), V((48, 256), bf16),
            V((24, 256), f32), V((256, 128), f32), V((FEAT, FH), f32),
            V((21, 256, 128), f32), V((256, 384), bf16), V((256, 18 * 128), f32),
            V((3, 256, 256), f32), V((21, 256, 256), bf16),
            V((3, 256, 256), f32), V((256, 768), bf16), V((FH, SEQ), f32),
            V((2 * FH, SEQ), bf16), V((512, 128), f32),
            V((512, 128), f32), V((512, 128), f32),
            V((OWN * K1, 256), f32), V((OWN * K1, 256), f32), V((OWN * K1, 256), f32),
            V((NCTX, 16, 256), bf16), V((NCTX, 16, 256), bf16),
            V((NCTX, 16, 256), bf16), V((NCTX, 16, 256), bf16),
            V((NCTX, 16, 256), bf16), V((NCTX, 16, 256), bf16),
            V((NCTX, 16, 256), bf16), V((NCTX, 16, 256), bf16),
            V((3 * OWN, SEQ), bf16), V((2 * FH, SEQ), bf16),
            V((21, 256, 256), bf16), V((2, 16, 256), bf16), V((2, NCTX, 16, 256), bf16),
            V((3, 8, 128), f32), V((NCTX, 8, 128), f32), V((chans, 8, 128), f32),
            V((3, 8, 128), f32), V((48, 128), f32),
            dma((2,)), dma((2,)), dma((NCTX,)), dma((NCTX,)), dma((NCTX,)), dma((NCTX,)),
            dma((NCTX,)), dma((NCTX,)), dma((NCTX,)), dma((NCTX,)),
            dma((2, NCTX)), dma((2, NCTX)), dma((3,)), dma((NCTX,)),
            dma((chans,)), dma((chans,)), dma((NCTX,)), dma((3,)),
        ],
        compiler_params=pltpu.CompilerParams(
            collective_id=0, has_side_effects=True, vmem_limit_bytes=56 * 1024 * 1024),
    )(*args)
    outs = pl.pallas_call(
        hand_on,
        out_shape=shapes,
        in_specs=[hbm] * 8,
        out_specs=[hbm] * 8,
        scratch_shapes=[V(a.shape, a.dtype) for a in shapes] + [dma((8,)), dma((8,))],
    )(*outs)
    return outs[:6] + (outs[6].T, outs[7].reshape(OWN))


def solution(mesh):
    consts = tables()
    return jax.shard_map(
        functools.partial(per_device, consts, mesh.shape["chan"]),
        mesh=mesh,
        in_specs=(
            P("chan", "ctx"),
            P("chan", "ctx"),
            P("chan", "ctx"),
            P("chan", "ctx"),
            P(None, None, "chan"),
            P(),
            P(None, ("chan", "ctx")),
            P(("chan", "ctx")),
            P(("chan", "ctx")),
        ),
        out_specs=(
            P("chan", "ctx"),
            P("chan", "ctx"),
            P("chan", "ctx"),
            P("chan", "ctx"),
            P(None, None, "chan"),
            P(),
            P(None, ("chan", "ctx")),
            P(("chan", "ctx")),
        ),
        check_vma=False,
    )
```

```python
import functools
import math

import jax
import jax.numpy as jnp
import ml_dtypes
import numpy as np
from jax import lax
from jax.experimental import pallas as pl
from jax.experimental.pallas import tpu as pltpu
from jax.sharding import PartitionSpec as P

D = 8192
SEQ = 4096
EMB = 33
FH = 64
TAPS = 7
NCTX = 16
POS = SEQ // NCTX
OWN = 16
K1 = 40
N1 = 64
N2 = 128
BLK = SEQ // N2
FEAT = 48
LOADS = 19
YS = 8
STEPS = sorted(((dx, dy) for dx in range(2) for dy in range(YS) if dx + dy > 0),
               key=lambda s: (-s[0] - min(s[1], YS - s[1]), s))
MESH = pl.DeviceIdType.MESH
f32 = jnp.float32
bf16 = jnp.bfloat16


def halves(x):
    x = np.asarray(x, np.float32)
    hi = x.astype(ml_dtypes.bfloat16)
    lo = (x - hi.astype(np.float32)).astype(ml_dtypes.bfloat16)
    return hi, lo


def tables():
    k1 = np.arange(K1)[:, None]
    live = (k1 <= N1 // 2).astype(np.float64)
    n = np.arange(BLK)[None, :]
    ang = 2 * np.pi * ((k1 * n) % N1) / N1
    c1 = np.concatenate([np.cos(ang) * live, -np.sin(ang) * live], 0)
    hi, lo = halves(c1)
    c1_two = np.concatenate([hi, lo], 1)
    c1_three = np.concatenate([hi, hi, lo], 1)
    weight = np.where((k1 == 0) | (k1 == N1 // 2), 1.0, 2.0) * live / (N1 * N2)
    d1 = np.concatenate([np.cos(ang) * weight, -np.sin(ang) * weight], 0).T
    hi, lo = halves(d1)
    d1_three = np.concatenate([hi, hi, lo], 1)
    m = np.arange(N2)
    turn = 2 * np.pi * ((m[:, None] * m[None, :]) % N2) / N2
    c, s = np.cos(turn), np.sin(turn)
    fwd = np.block([[c, -s], [s, c]])
    hi, lo = halves(fwd)
    fwd_three = np.concatenate([hi, hi, lo], 0)
    hi, lo = halves(fwd.T)
    inv_three = np.concatenate([hi, hi, lo], 0)
    twist = 2 * np.pi * ((k1 * m[None, :]) % (N1 * N2)) / (N1 * N2)
    twist = np.concatenate([np.cos(twist), np.sin(twist)], 0).astype(np.float32)
    t = np.arange(SEQ)
    bands = (EMB - 1) // 2
    b = np.arange(1, bands + 1)
    phase = 2 * np.pi * ((b[:, None] * t[None, :]) % SEQ) / SEQ
    feat = np.zeros((FEAT, SEQ))
    feat[0] = t / SEQ
    feat[1 : 1 + bands] = np.cos(phase)
    feat[1 + bands : 1 + 2 * bands] = np.sin(phase)
    feat_two = np.concatenate(halves(feat), 0)
    tail = np.zeros((32, 3 * 128), np.float32)
    head = np.zeros((48, 6 * 128), np.float32)
    place = np.zeros((48, 18 * 128), np.float32)
    for i in range(3):
        for r in range(8):
            tail[i * 8 + r, i * 128 + 120 + r] = 1
            for h in range(2):
                head[i * 16 + h * 8 + r, (i * 2 + h) * 128 + r] = 1
                for j in range(r + 1, TAPS):
                    place[i * 16 + h * 8 + r, (i * 6 + j - 1) * 128 + 128 + r - j] = 1
    as16 = lambda x: x.astype(ml_dtypes.bfloat16)
    return (c1_two, c1_three, d1_three, fwd_three, inv_three, twist, feat_two,
            as16(tail), as16(head), as16(place))


def split(x):
    hi = x.astype(bf16)
    return hi, (x - hi.astype(f32)).astype(bf16)


def mm(a, b, ca=1, cb=0):
    return lax.dot_general(a, b, (((ca,), (cb,)), ((), ())), preferred_element_type=f32)


def sin_cos(x):
    n = jnp.floor(x * (1.0 / math.pi) + 0.5)
    r = x - n * 3.140625
    r = r - n * 9.67502593994140625e-4
    r = r - n * 1.509957990978376e-7
    sign = 1.0 - 2.0 * (n - 2.0 * jnp.floor(n * 0.5))
    z = r * r
    s = -1.0 / 39916800.0
    for k in (1.0 / 362880.0, -1.0 / 5040.0, 1.0 / 120.0, -1.0 / 6.0, 1.0):
        s = s * z + k
    c = 1.0 / 479001600.0
    for k in (-1.0 / 3628800.0, 1.0 / 40320.0, -1.0 / 720.0, 1.0 / 24.0, -0.5, 1.0):
        c = c * z + k
    return s * r * sign, c * sign


def kernel(chans,
           *refs):
    sources, refs = refs[:LOADS], refs[LOADS:]
    targets, refs = refs[:8], refs[8:]
    held, refs = refs[:LOADS], refs[LOADS:]
    done, refs = refs[:8], refs[8:]
    (q_ref, k_ref, v_ref, cot_ref, taps_ref, fin_ref, fout_ref, decay_ref, skip_ref,
     c1_two, c1_three, d1_three, fwd_three, inv_three, twist, feat,
     tail_sel, head_sel, head_place) = held
    mixed_ref, qg_ref, kg_ref, vg_ref, tg_ref, fig_ref, fog_ref, sg_ref = done
    (load_s, store_s, tails_out, tails_in, heads_out, heads_in, tap_rows, tap_cols, fin_pad,
     tap_wide, prev, after, shorts, shifted, grads, ahead, bend, act, env,
     sig, sig_u, spec_h, spec_u, spec_g,
     u_out, u_in, g_out, g_in, conv_out, conv_in, back_out, back_in, bent, slope,
     prods, tap_out, tap_in, in_tiles, in_parts, in_row, in_sums, in_flat,
     halo_s, halo_r, u_s, u_r, g_s, g_r, conv_s, conv_r, back_s, back_r,
     tp_s, tp_r, ip_s, ip_r, iq_s, iq_r, is_s, is_r) = refs
    me = lax.axis_index("ctx")
    ch = lax.axis_index("chan")
    quads = math.gcd(chans, 4)
    stacks = chans // quads
    chan_steps = sorted(((dz, dw) for dz in range(stacks) for dw in range(quads) if dz + dw > 0),
                        key=lambda s: (-min(s[0], stacks - s[0]) - s[1] // 2, s))

    def at(ctx_index):
        return {"ctx": ctx_index, "chan": ch}

    def over(chan_index):
        return {"ctx": me, "chan": chan_index}

    def copy(src, dst, send, recv, where):
        return pltpu.make_async_remote_copy(
            src_ref=src, dst_ref=dst, send_sem=send, recv_sem=recv,
            device_id=where, device_id_type=MESH)

    def each(count, body, start=1):
        for d in range(start, count):
            body(d)

    def other(d):
        return lax.rem(me + d, NCTX)

    def peers(body):
        for dx, dy in STEPS:
            body(lax.rem(me // YS + dx, NCTX // YS) * YS + lax.rem(me % YS + dy, YS))

    def chan_peers(body):
        for n, (dz, dw) in enumerate(chan_steps):
            body(n, lax.rem(ch // quads + dz, stacks) * quads + (ch % quads ^ dw))

    in_owner = jnp.logical_and(lax.rem(me, 2) == 1, me < 6)
    in_index = jnp.minimum(me // 2, 2)

    barrier = pltpu.get_barrier_semaphore()

    def greet(where):
        pl.semaphore_signal(barrier, inc=1, device_id=where, device_id_type=MESH)

    peers(lambda p: greet(at(p)))

    @pl.when(in_owner)
    def _():
        chan_peers(lambda n, p: greet(over(p)))

    def load(k):
        return pltpu.make_async_copy(sources[k], held[k], load_s.at[k])

    def store(k):
        return pltpu.make_async_copy(done[k], targets[k], store_s.at[k])

    for k in (0, 1, 2, 16, 4, 5, 15, 3, 6, 7, 8, 14, 10, 12, 9, 11, 13, 17, 18):
        load(k).start()

    for k in (0, 1, 2, 16):
        load(k).wait()
    ends = jnp.concatenate([r[:, 128:256] for r in (q_ref, k_ref, v_ref)], axis=1)
    tails_out[...] = mm(tail_sel[...], ends, 1, 1).astype(bf16)
    pl.semaphore_wait(barrier, jnp.where(in_owner, NCTX - 1 + chans - 1, NCTX - 1))
    tail_copy = copy(tails_out, tails_in, halo_s.at[0], halo_r.at[0], at(other(1)))
    tail_copy.start()

    load(4).wait()
    tap_rows[...] = jnp.zeros_like(tap_rows)
    for i in range(3):
        tap_rows[i * 8 : i * 8 + TAPS, :] = taps_ref[i]
    row = lax.broadcasted_iota(jnp.int32, (24, 128), 0)
    col = lax.broadcasted_iota(jnp.int32, (24, 128), 1)
    unit = (row == col).astype(bf16)
    hi, lo = split(tap_rows[...])
    rest = (tap_rows[...] - hi.astype(f32) - lo.astype(f32)).astype(bf16)
    tap_cols[...] = mm(hi, unit, 0, 0) + mm(lo, unit, 0, 0) + mm(rest, unit, 0, 0)
    ROWS = 32
    CHUNKS = 256 // ROWS

    def spread(d):
        rows = pl.ds(d * ROWS, ROWS)
        for i in range(3):
            for j in range(TAPS):
                one = tap_cols[rows, i * 8 + j : i * 8 + j + 1]
                tap_wide[i * TAPS + j, rows, :] = jnp.broadcast_to(one, (ROWS, 128))

    each(CHUNKS, spread, 0)

    load(5).wait()
    load(15).wait()
    fin_pad[...] = jnp.zeros_like(fin_pad)
    fin_pad[0:EMB, :] = fin_ref[...]
    fin_hi, fin_lo = split(fin_pad[...])
    fin_three = jnp.concatenate([fin_hi, fin_hi, fin_lo], axis=0)
    WIDE = 512

    def network(d):
        cols = pl.ds(d * WIDE, WIDE)
        f = feat[:, cols]
        pre = mm(fin_three, jnp.concatenate([f, f[0:FEAT, :]], axis=0), 0, 0)
        s, c = sin_cos(pre)
        bend[:, cols] = c
        a, b = split(s)
        act[0:FH, cols] = a
        act[FH : 2 * FH, cols] = b

    each(SEQ // WIDE, network, 0)

    tail_copy.wait_recv()
    inside = jnp.where(me > 0, 1.0, 0.0)
    prev[...] = (mm(tails_in[...], tail_sel[...], 0, 0) * inside).astype(bf16)

    def moved(x, by):
        return x if by == 0 else pltpu.roll(x, by, 1)

    def short(i, ref, rows):
        x = jnp.concatenate([prev[rows, i * 128 : (i + 1) * 128], ref[rows, :]], axis=1)
        acc = None
        for j in range(TAPS):
            y = moved(x, j)[:, 128:384]
            shifted[i * TAPS + j, rows, :] = y
            tap = tap_wide[i * TAPS + j, rows, :]
            term = jnp.concatenate([tap, tap], axis=1) * y.astype(f32)
            acc = term if acc is None else acc + term
        shorts[i, rows, :] = acc
        return acc

    def scatter(out, inn, send, recv):
        inn[me] = out[me]
        peers(lambda p: copy(out.at[p], inn.at[me], send.at[p], recv.at[me], at(p)).start())

    def short_part(which, out):
        for part in range(CHUNKS):
            rows = pl.ds(part * ROWS, ROWS)
            if which == 0:
                x = short(1, k_ref, rows) * short(2, v_ref, rows)
            else:
                x = cot_ref[rows, :].astype(f32) * short(0, q_ref, rows)
            for h in range(2):
                out[part * 2 + h] = x[h * 16 : (h + 1) * 16, :].astype(bf16)

    short_part(0, u_out)
    scatter(u_out, u_in, u_s, u_r)
    load(3).wait()
    short_part(1, g_out)
    scatter(g_out, g_in, g_s, g_r)

    for k in (6, 7, 8):
        load(k).wait()
    eye = (lax.broadcasted_iota(jnp.int32, (OWN, OWN), 0)
           == lax.broadcasted_iota(jnp.int32, (OWN, OWN), 1)).astype(f32)
    decay = jnp.sum(eye * decay_ref[...], axis=1, keepdims=True)
    skip = jnp.sum(eye * skip_ref[...], axis=1, keepdims=True)
    w_hi, w_lo = split(fout_ref[...])
    w_two = jnp.concatenate([w_hi, w_lo], axis=0)
    w_three = jnp.concatenate([w_hi, w_hi, w_lo], axis=0)
    scale = 1.0 / math.sqrt(SEQ)

    def filters(d):
        cols = pl.ds(d * WIDE, WIDE)
        raw = mm(w_two, act[0:FH, cols])
        raw = raw[0:OWN, :] + raw[OWN : 2 * OWN, :] + mm(w_hi, act[FH : 2 * FH, cols])
        t = (d * WIDE + lax.broadcasted_iota(jnp.int32, (OWN, WIDE), 1)).astype(f32)
        e = jnp.exp(-decay * (t * (1.0 / SEQ))) * scale
        h = raw * e
        for n in range(WIDE // 128):
            rows = pl.ds((d * (WIDE // 128) + n) * OWN, OWN)
            env[rows, :] = e[:, n * 128 : (n + 1) * 128]
            sig[rows, :] = h[:, n * 128 : (n + 1) * 128]

    each(SEQ // WIDE, filters, 0)

    for k in (9, 10, 11, 12, 13, 14):
        load(k).wait()
    GRP = 4
    tc, ts = twist[0:K1, :], twist[K1 : 2 * K1, :]

    def three(x, axis):
        hi, lo = split(x)
        return jnp.concatenate([hi, lo, hi], axis=axis)

    def forward(src, spec, exact):
        for grp in range(OWN // GRP):
            x = jnp.concatenate(
                [src[pl.ds(grp * GRP + c, BLK, stride=OWN), :] for c in range(GRP)], axis=1)
            if exact:
                x = x.astype(bf16)
                a = mm(c1_two[...], jnp.concatenate([x, x], axis=0))
            else:
                a = mm(c1_three[...], three(x, 0))
            re, im = [], []
            for c in range(GRP):
                ar = a[0:K1, c * 128 : (c + 1) * 128]
                ai = a[K1 : 2 * K1, c * 128 : (c + 1) * 128]
                re.append(ar * tc + ai * ts)
                im.append(ai * tc - ar * ts)
            x = jnp.concatenate([jnp.concatenate(re, 0), jnp.concatenate(im, 0)], axis=1)
            spec[grp * GRP * K1 : (grp + 1) * GRP * K1, :] = mm(three(x, 1), fwd_three[...])

    def backward(first, second, conj, dst):
        for grp in range(OWN // GRP):
            rows = slice(grp * GRP * K1, (grp + 1) * GRP * K1)
            ar, ai = first[rows, 0:128], first[rows, 128:256]
            br, bi = second[rows, 0:128], second[rows, 128:256]
            if conj:
                y = [ar * br + ai * bi, ai * br - ar * bi]
            else:
                y = [ar * br - ai * bi, ar * bi + ai * br]
            z = mm(three(jnp.concatenate(y, axis=1), 1), inv_three[...])
            out = []
            for c in range(GRP):
                zr = z[c * K1 : (c + 1) * K1, 0:128]
                zi = z[c * K1 : (c + 1) * K1, 128:256]
                out.append(jnp.concatenate([zr * tc - zi * ts, zi * tc + zr * ts], axis=0))
            r = mm(d1_three[...], three(jnp.concatenate(out, axis=1), 0))
            for c in range(GRP):
                dst[pl.ds(grp * GRP + c, BLK, stride=OWN), :] = r[:, c * 128 : (c + 1) * 128]

    forward(sig, spec_h, False)

    def wait_all(out, inn, send, recv):
        peers(lambda p: copy(out.at[p], inn.at[p], send.at[p], recv.at[p], at(p)).wait_recv())

    def unfold(inn, dst):
        for n in range(BLK):
            half = n % 2 * 128
            dst[n * 16 : (n + 1) * 16, :] = inn[n // 2, :, half : half + 128].astype(f32)

    def fold(result, direct, out):
        for s in range(NCTX):
            x = jnp.concatenate(
                [result[(2 * s + h) * 16 : (2 * s + h + 1) * 16, :] for h in range(2)], axis=1)
            out[s] = (x + skip * direct[s].astype(f32)).astype(bf16)

    wait_all(u_out, u_in, u_s, u_r)
    unfold(u_in, sig_u)
    forward(sig_u, spec_u, True)
    backward(spec_u, spec_h, False, sig_u)
    fold(sig_u, u_in, conv_out)
    scatter(conv_out, conv_in, conv_s, conv_r)
    wait_all(g_out, g_in, g_s, g_r)
    unfold(g_in, sig)
    forward(sig, spec_g, True)

    backward(spec_g, spec_u, True, sig)
    sg_ref[...] = jnp.sum(eye * sig[0:16, 0:1], axis=0, keepdims=True) * scale
    store(7).start()
    for n in range(BLK):
        cols = slice(n * 128, (n + 1) * 128)
        a, b = split(sig[n * 16 : (n + 1) * 16, :] * env[n * 16 : (n + 1) * 16, :])
        bent[0:16, cols] = a
        bent[16:32, cols] = b
        bent[32:48, cols] = a
    def slopes(d):
        cols = pl.ds(d * 2 * WIDE, 2 * WIDE)
        a, b = split(mm(w_three, bent[:, cols], 0, 0) * bend[:, cols])
        slope[0:FH, cols] = a
        slope[FH : 2 * FH, cols] = b

    each(SEQ // (2 * WIDE), slopes, 0)
    total = mm(feat[...], slope[...], 1, 1)
    in_sum = (total[0:FEAT, :] + total[FEAT : 2 * FEAT, :] + pltpu.roll(total[0:FEAT, :], FH, 1))
    in_flat[...] = jnp.zeros_like(in_flat)
    in_flat[:, 0:FH] = in_sum[:, 0:FH]
    packed = in_flat[0:24, :] + pltpu.roll(in_flat[24:48, :], 64, 1)
    for k in range(3):
        in_tiles[k] = packed[k * 8 : (k + 1) * 8, :]

    def deal(go):
        for k in range(3):
            @pl.when(me != 2 * k + 1)
            def _(k=k):
                go(copy(in_tiles.at[k], in_parts.at[me], ip_s.at[k], ip_r.at[me], at(2 * k + 1)))

    deal(lambda c: c.start())
    backward(spec_g, spec_h, True, sig)
    fold(sig, g_in, back_out)
    scatter(back_out, back_in, back_s, back_r)
    total = mm(bent[0:32, :], act[...], 1, 1)
    fog_ref[...] = (total[0:OWN, 0:FH] + total[OWN : 2 * OWN, 0:FH]
                    + pltpu.roll(total[0:OWN, :], FH, 1)[:, 0:FH]) * scale
    store(6).start()

    def take(i, g, rows):
        grads[i, rows, :] = g
        hi, lo = split(g[:, 0:128])
        ahead[rows, i * 256 : i * 256 + 128] = hi
        ahead[rows, i * 256 + 128 : i * 256 + 256] = lo
        for j in range(TAPS):
            x = g * shifted[i * TAPS + j, rows, :].astype(f32)
            hi, lo = split(x[:, 0:128] + x[:, 128:256])
            prods[i * TAPS + j, rows, 0:128] = hi
            prods[i * TAPS + j, rows, 128:256] = lo

    pick_row = lax.broadcasted_iota(jnp.int32, (16, 256), 0)

    def tap_sum(k, which):
        total = jnp.zeros((16, 256), f32)
        for n, i in enumerate(which):
            for j in range(TAPS):
                pick = (pick_row == n * 8 + j).astype(f32).astype(bf16)
                total = total + mm(pick, prods[i * TAPS + j], 1, 1)
        tap_out[k] = total.astype(bf16)
        tap_in[k, me] = tap_out[k]
        peers(lambda p: copy(tap_out.at[k], tap_in.at[k, me], tp_s.at[k, p], tp_r.at[k, me],
                             at(p)).start())

    def conv_part(d):
        rows = pl.ds(d * ROWS, ROWS)
        cv = jnp.concatenate([conv_in[2 * d], conv_in[2 * d + 1]], axis=0).astype(f32)
        mixed_ref[rows, :] = (shorts[0, rows, :] * cv).astype(bf16)
        take(0, cot_ref[rows, :].astype(f32) * cv, rows)

    def back_part(d):
        rows = pl.ds(d * ROWS, ROWS)
        bk = jnp.concatenate([back_in[2 * d], back_in[2 * d + 1]], axis=0).astype(f32)
        take(1, bk * shorts[2, rows, :], rows)
        take(2, bk * shorts[1, rows, :], rows)

    wait_all(conv_out, conv_in, conv_s, conv_r)
    each(CHUNKS, conv_part, 0)
    store(0).start()
    tap_sum(0, (0,))

    @pl.when(in_owner)
    def _():
        peers(lambda p: copy(in_tiles.at[0], in_parts.at[p], ip_r.at[p], ip_r.at[p],
                             at(p)).wait_recv())
        in_parts[me] = in_tiles[in_index]
        t = in_parts[0]
        for p in range(1, NCTX):
            t = t + in_parts[p]
        in_row[ch] = t
        chan_peers(lambda n, p: copy(in_row.at[ch], in_row.at[ch], iq_s.at[n], iq_r.at[ch],
                                     over(p)).start())

    load(17).wait()
    load(18).wait()
    wait_all(back_out, back_in, back_s, back_r)
    each(CHUNKS, back_part, 0)
    tap_sum(1, (1, 2))
    heads_out[...] = mm(head_sel[...], ahead[...], 1, 1).astype(bf16)
    head_copy = copy(heads_out, heads_in, halo_s.at[1], halo_r.at[1], at(other(NCTX - 1)))
    head_copy.start()

    head_copy.wait_recv()
    before_end = jnp.where(me < NCTX - 1, 1.0, 0.0)
    after[...] = mm(heads_in[...], head_place[...], 0, 0) * before_end
    lane = lax.broadcasted_iota(jnp.int32, (ROWS, 128), 1)

    def proj(i, ref):
        def proj_part(d):
            rows = slice(d * ROWS, (d + 1) * ROWS)
            left, right = grads[i, rows, 0:128], grads[i, rows, 128:256]
            tap = tap_wide[i * TAPS, rows, :]
            acc = [tap * left, tap * right]
            for j in range(1, TAPS):
                tap = tap_wide[i * TAPS + j, rows, :]
                near, far = pltpu.roll(left, 128 - j, 1), pltpu.roll(right, 128 - j, 1)
                edge = after[rows, (i * 6 + j - 1) * 128 : (i * 6 + j) * 128]
                here = lane < 128 - j
                acc[0] = acc[0] + tap * jnp.where(here, near, far)
                acc[1] = acc[1] + tap * jnp.where(here, far, edge)
            ref[rows, 0:128] = acc[0].astype(bf16)
            ref[rows, 128:256] = acc[1].astype(bf16)

        for d in range(CHUNKS):
            proj_part(d)
        store(1 + i).start()

    proj(0, qg_ref)
    proj(1, kg_ref)
    proj(2, vg_ref)

    @pl.when(in_owner)
    def _():
        chan_peers(lambda n, p: copy(in_row.at[p], in_row.at[p], iq_s.at[n], iq_r.at[p],
                                     over(p)).wait_recv())
        t = in_row[0]
        for p in range(1, chans):
            t = t + in_row[p]
        in_sums[in_index] = t
        peers(lambda p: copy(in_sums.at[in_index], in_sums.at[in_index], is_s.at[p],
                             is_r.at[in_index], at(p)).start())

    for k in range(2):
        peers(lambda p: copy(tap_out.at[k], tap_in.at[k, p], tp_s.at[k, p], tp_r.at[k, p],
                             at(p)).wait_recv())
        t = tap_in[k, 0].astype(f32)
        for p in range(1, NCTX):
            t = t + tap_in[k, p].astype(f32)
        if k == 0:
            tg_ref[0] = t[0:TAPS, :] * scale
        else:
            tg_ref[1] = t[0:TAPS, :] * scale
            tg_ref[2] = t[8 : 8 + TAPS, :] * scale
    store(4).start()
    for k in range(3):
        @pl.when(me != 2 * k + 1)
        def _(k=k):
            copy(in_sums.at[k], in_sums.at[k], is_s.at[0], is_r.at[k], at(2 * k + 1)).wait_recv()
    sums = jnp.concatenate([in_sums[k] for k in range(3)], axis=0) * (scale / math.sqrt(D))
    fig_ref[0:24, :] = sums[:, 0:FH]
    fig_ref[24:EMB, :] = pltpu.roll(sums, 64, 1)[0 : EMB - 24, 0:FH]
    store(5).start()

    for k in range(8):
        store(k).wait()
    tail_copy.wait_send()
    head_copy.wait_send()
    deal(lambda c: c.wait_send())

    def left(p):
        for out, inn, send, recv in ((u_out, u_in, u_s, u_r), (g_out, g_in, g_s, g_r),
                                     (conv_out, conv_in, conv_s, conv_r),
                                     (back_out, back_in, back_s, back_r)):
            copy(out.at[p], inn.at[me], send.at[p], recv.at[me], at(p)).wait_send()
        for k in range(2):
            copy(tap_out.at[k], tap_in.at[k, me], tp_s.at[k, p], tp_r.at[k, me], at(p)).wait_send()

    peers(left)

    @pl.when(in_owner)
    def _():
        chan_peers(lambda n, p: copy(in_row.at[ch], in_row.at[ch], iq_s.at[n], iq_r.at[ch],
                                     over(p)).wait_send())
        peers(lambda p: copy(in_sums.at[in_index], in_sums.at[in_index], is_s.at[p],
                             is_r.at[in_index], at(p)).wait_send())


def hand_on(*refs):
    held, load_s, store_s = refs[16:24], refs[24], refs[25]
    loads = [pltpu.make_async_copy(refs[k], held[k], load_s.at[k]) for k in range(8)]
    stores = [pltpu.make_async_copy(held[k], refs[8 + k], store_s.at[k]) for k in range(8)]
    for c in loads:
        c.start()
    for k in range(8):
        loads[k].wait()
        stores[k].start()
    for c in stores:
        c.wait()


def per_device(consts, chans, query_proj, key_proj, value_proj, out_cotangent, short_taps,
               filter_in, filter_out, decay_rate, skip_gain):
    block = jax.ShapeDtypeStruct((256, POS), bf16)
    dma = pltpu.SemaphoreType.DMA
    V = pltpu.VMEM
    args = [query_proj, key_proj, value_proj, out_cotangent, short_taps, filter_in, filter_out.T,
            decay_rate.reshape(1, OWN), skip_gain.reshape(1, OWN)]
    args += [jnp.asarray(c) for c in consts]
    shapes = (block, block, block, block,
              jax.ShapeDtypeStruct((3, TAPS, 256), f32),
              jax.ShapeDtypeStruct((EMB, FH), f32),
              jax.ShapeDtypeStruct((OWN, FH), f32),
              jax.ShapeDtypeStruct((1, OWN), f32))
    hbm = pl.BlockSpec(memory_space=pl.ANY)
    outs = pl.pallas_call(
        functools.partial(kernel, chans),
        out_shape=shapes,
        in_specs=[hbm] * LOADS,
        out_specs=[hbm] * 8,
        scratch_shapes=[V(a.shape, a.dtype) for a in args] + [V(a.shape, a.dtype) for a in shapes] + [
            dma((LOADS,)), dma((8,)),
            V((32, 256), bf16), V((32, 256), bf16), V((48, 256), bf16), V((48, 256), bf16),
            V((24, 256), f32), V((256, 128), f32), V((FEAT, FH), f32),
            V((21, 256, 128), f32), V((256, 384), bf16), V((256, 18 * 128), f32),
            V((3, 256, 256), f32), V((21, 256, 256), bf16),
            V((3, 256, 256), f32), V((256, 768), bf16), V((FH, SEQ), f32),
            V((2 * FH, SEQ), bf16), V((512, 128), f32),
            V((512, 128), f32), V((512, 128), f32),
            V((OWN * K1, 256), f32), V((OWN * K1, 256), f32), V((OWN * K1, 256), f32),
            V((NCTX, 16, 256), bf16), V((NCTX, 16, 256), bf16),
            V((NCTX, 16, 256), bf16), V((NCTX, 16, 256), bf16),
            V((NCTX, 16, 256), bf16), V((NCTX, 16, 256), bf16),
            V((NCTX, 16, 256), bf16), V((NCTX, 16, 256), bf16),
            V((3 * OWN, SEQ), bf16), V((2 * FH, SEQ), bf16),
            V((21, 256, 256), bf16), V((2, 16, 256), bf16), V((2, NCTX, 16, 256), bf16),
            V((3, 8, 128), f32), V((NCTX, 8, 128), f32), V((chans, 8, 128), f32),
            V((3, 8, 128), f32), V((48, 128), f32),
            dma((2,)), dma((2,)), dma((NCTX,)), dma((NCTX,)), dma((NCTX,)), dma((NCTX,)),
            dma((NCTX,)), dma((NCTX,)), dma((NCTX,)), dma((NCTX,)),
            dma((2, NCTX)), dma((2, NCTX)), dma((3,)), dma((NCTX,)),
            dma((chans,)), dma((chans,)), dma((NCTX,)), dma((3,)),
        ],
        compiler_params=pltpu.CompilerParams(
            collective_id=0, has_side_effects=True, vmem_limit_bytes=56 * 1024 * 1024),
    )(*args)
    outs = pl.pallas_call(
        hand_on,
        out_shape=shapes,
        in_specs=[hbm] * 8,
        out_specs=[hbm] * 8,
        scratch_shapes=[V(a.shape, a.dtype) for a in shapes] + [dma((8,)), dma((8,))],
    )(*outs)
    return outs[:6] + (outs[6].T, outs[7].reshape(OWN))


def solution(mesh):
    consts = tables()
    return jax.shard_map(
        functools.partial(per_device, consts, mesh.shape["chan"]),
        mesh=mesh,
        in_specs=(
            P("chan", "ctx"),
            P("chan", "ctx"),
            P("chan", "ctx"),
            P("chan", "ctx"),
            P(None, None, "chan"),
            P(),
            P(None, ("chan", "ctx")),
            P(("chan", "ctx")),
            P(("chan", "ctx")),
        ),
        out_specs=(
            P("chan", "ctx"),
            P("chan", "ctx"),
            P("chan", "ctx"),
            P("chan", "ctx"),
            P(None, None, "chan"),
            P(),
            P(None, ("chan", "ctx")),
            P(("chan", "ctx")),
        ),
        check_vma=False,
    )
```

```python
import functools
import math

import jax
import jax.numpy as jnp
import ml_dtypes
import numpy as np
from jax import lax
from jax.experimental import pallas as pl
from jax.experimental.pallas import tpu as pltpu
from jax.sharding import PartitionSpec as P

D = 8192
SEQ = 4096
EMB = 33
FH = 64
TAPS = 7
NCTX = 16
POS = SEQ // NCTX
OWN = 16
K1 = 40
N1 = 64
N2 = 128
BLK = SEQ // N2
FEAT = 48
LOADS = 19
YS = 8
STEPS = sorted(((dx, dy) for dx in range(2) for dy in range(YS) if dx + dy > 0),
               key=lambda s: (-s[0] - min(s[1], YS - s[1]), s))
MESH = pl.DeviceIdType.MESH
f32 = jnp.float32
bf16 = jnp.bfloat16


def halves(x):
    x = np.asarray(x, np.float32)
    hi = x.astype(ml_dtypes.bfloat16)
    lo = (x - hi.astype(np.float32)).astype(ml_dtypes.bfloat16)
    return hi, lo


def tables():
    k1 = np.arange(K1)[:, None]
    live = (k1 <= N1 // 2).astype(np.float64)
    n = np.arange(BLK)[None, :]
    ang = 2 * np.pi * ((k1 * n) % N1) / N1
    c1 = np.concatenate([np.cos(ang) * live, -np.sin(ang) * live], 0)
    hi, lo = halves(c1)
    c1_two = np.concatenate([hi, lo], 1)
    c1_three = np.concatenate([hi, hi, lo], 1)
    weight = np.where((k1 == 0) | (k1 == N1 // 2), 1.0, 2.0) * live / (N1 * N2)
    d1 = np.concatenate([np.cos(ang) * weight, -np.sin(ang) * weight], 0).T
    hi, lo = halves(d1)
    d1_three = np.concatenate([hi, hi, lo], 1)
    m = np.arange(N2)
    turn = 2 * np.pi * ((m[:, None] * m[None, :]) % N2) / N2
    c, s = np.cos(turn), np.sin(turn)
    fwd = np.block([[c, -s], [s, c]])
    hi, lo = halves(fwd)
    fwd_three = np.concatenate([hi, hi, lo], 0)
    hi, lo = halves(fwd.T)
    inv_three = np.concatenate([hi, hi, lo], 0)
    twist = 2 * np.pi * ((k1 * m[None, :]) % (N1 * N2)) / (N1 * N2)
    twist = np.concatenate([np.cos(twist), np.sin(twist)], 0).astype(np.float32)
    t = np.arange(SEQ)
    bands = (EMB - 1) // 2
    b = np.arange(1, bands + 1)
    phase = 2 * np.pi * ((b[:, None] * t[None, :]) % SEQ) / SEQ
    feat = np.zeros((FEAT, SEQ))
    feat[0] = t / SEQ
    feat[1 : 1 + bands] = np.cos(phase)
    feat[1 + bands : 1 + 2 * bands] = np.sin(phase)
    feat_two = np.concatenate(halves(feat), 0)
    tail = np.zeros((32, 3 * 128), np.float32)
    head = np.zeros((48, 6 * 128), np.float32)
    place = np.zeros((48, 18 * 128), np.float32)
    for i in range(3):
        for r in range(8):
            tail[i * 8 + r, i * 128 + 120 + r] = 1
            for h in range(2):
                head[i * 16 + h * 8 + r, (i * 2 + h) * 128 + r] = 1
                for j in range(r + 1, TAPS):
                    place[i * 16 + h * 8 + r, (i * 6 + j - 1) * 128 + 128 + r - j] = 1
    as16 = lambda x: x.astype(ml_dtypes.bfloat16)
    return (c1_two, c1_three, d1_three, fwd_three, inv_three, twist, feat_two,
            as16(tail), as16(head), as16(place))


def split(x):
    hi = x.astype(bf16)
    return hi, (x - hi.astype(f32)).astype(bf16)


def mm(a, b, ca=1, cb=0):
    return lax.dot_general(a, b, (((ca,), (cb,)), ((), ())), preferred_element_type=f32)


def sin_cos(x):
    n = jnp.floor(x * (1.0 / math.pi) + 0.5)
    r = x - n * 3.140625
    r = r - n * 9.67502593994140625e-4
    r = r - n * 1.509957990978376e-7
    sign = 1.0 - 2.0 * (n - 2.0 * jnp.floor(n * 0.5))
    z = r * r
    s = -1.0 / 39916800.0
    for k in (1.0 / 362880.0, -1.0 / 5040.0, 1.0 / 120.0, -1.0 / 6.0, 1.0):
        s = s * z + k
    c = 1.0 / 479001600.0
    for k in (-1.0 / 3628800.0, 1.0 / 40320.0, -1.0 / 720.0, 1.0 / 24.0, -0.5, 1.0):
        c = c * z + k
    return s * r * sign, c * sign


def kernel(chans,
           *refs):
    sources, refs = refs[:LOADS], refs[LOADS:]
    targets, refs = refs[:8], refs[8:]
    held, refs = refs[:LOADS], refs[LOADS:]
    done, refs = refs[:8], refs[8:]
    (q_ref, k_ref, v_ref, cot_ref, taps_ref, fin_ref, fout_ref, decay_ref, skip_ref,
     c1_two, c1_three, d1_three, fwd_three, inv_three, twist, feat,
     tail_sel, head_sel, head_place) = held
    mixed_ref, qg_ref, kg_ref, vg_ref, tg_ref, fig_ref, fog_ref, sg_ref = done
    (load_s, store_s, tails_out, tails_in, heads_out, heads_in, tap_rows, tap_cols, fin_pad,
     tap_wide, prev, after, shorts, shifted, grads, ahead, bend, act, env,
     sig, sig_u, spec_h, spec_u, spec_g,
     u_out, u_in, g_out, g_in, conv_out, conv_in, back_out, back_in, bent, slope,
     prods, tap_out, tap_in, in_tiles, in_parts, in_row, in_sums, in_flat,
     halo_s, halo_r, u_s, u_r, g_s, g_r, conv_s, conv_r, back_s, back_r,
     tp_s, tp_r, ip_s, ip_r, iq_s, iq_r, is_s, is_r) = refs
    me = lax.axis_index("ctx")
    ch = lax.axis_index("chan")
    quads = math.gcd(chans, 4)
    stacks = chans // quads
    chan_steps = sorted(((dz, dw) for dz in range(stacks) for dw in range(quads) if dz + dw > 0),
                        key=lambda s: (-min(s[0], stacks - s[0]) - s[1] // 2, s))

    def at(ctx_index):
        return {"ctx": ctx_index, "chan": ch}

    def over(chan_index):
        return {"ctx": me, "chan": chan_index}

    def copy(src, dst, send, recv, where):
        return pltpu.make_async_remote_copy(
            src_ref=src, dst_ref=dst, send_sem=send, recv_sem=recv,
            device_id=where, device_id_type=MESH)

    def each(count, body, start=1):
        for d in range(start, count):
            body(d)

    def other(d):
        return lax.rem(me + d, NCTX)

    def peers(body):
        for dx, dy in STEPS:
            body(lax.rem(me // YS + dx, NCTX // YS) * YS + lax.rem(me % YS + dy, YS))

    def chan_peers(body):
        for n, (dz, dw) in enumerate(chan_steps):
            body(n, lax.rem(ch // quads + dz, stacks) * quads + (ch % quads ^ dw))

    in_owner = jnp.logical_and(lax.rem(me, 2) == 1, me < 6)
    in_index = jnp.minimum(me // 2, 2)

    barrier = pltpu.get_barrier_semaphore()

    def greet(where):
        pl.semaphore_signal(barrier, inc=1, device_id=where, device_id_type=MESH)

    peers(lambda p: greet(at(p)))

    @pl.when(in_owner)
    def _():
        chan_peers(lambda n, p: greet(over(p)))

    def load(k):
        return pltpu.make_async_copy(sources[k], held[k], load_s.at[k])

    def store(k):
        return pltpu.make_async_copy(done[k], targets[k], store_s.at[k])

    for k in (0, 1, 2, 16, 4, 5, 15, 3, 6, 7, 8, 14, 10, 12, 9, 11, 13, 17, 18):
        load(k).start()

    for k in (0, 1, 2, 16):
        load(k).wait()
    ends = jnp.concatenate([r[:, 128:256] for r in (q_ref, k_ref, v_ref)], axis=1)
    tails_out[...] = mm(tail_sel[...], ends, 1, 1).astype(bf16)
    pl.semaphore_wait(barrier, jnp.where(in_owner, NCTX - 1 + chans - 1, NCTX - 1))
    tail_copy = copy(tails_out, tails_in, halo_s.at[0], halo_r.at[0], at(other(1)))
    tail_copy.start()

    load(4).wait()
    tap_rows[...] = jnp.zeros_like(tap_rows)
    for i in range(3):
        tap_rows[i * 8 : i * 8 + TAPS, :] = taps_ref[i]
    row = lax.broadcasted_iota(jnp.int32, (24, 128), 0)
    col = lax.broadcasted_iota(jnp.int32, (24, 128), 1)
    unit = (row == col).astype(bf16)
    hi, lo = split(tap_rows[...])
    rest = (tap_rows[...] - hi.astype(f32) - lo.astype(f32)).astype(bf16)
    tap_cols[...] = mm(hi, unit, 0, 0) + mm(lo, unit, 0, 0) + mm(rest, unit, 0, 0)
    ROWS = 32
    CHUNKS = 256 // ROWS

    def spread(d):
        rows = pl.ds(d * ROWS, ROWS)
        for i in range(3):
            for j in range(TAPS):
                one = tap_cols[rows, i * 8 + j : i * 8 + j + 1]
                tap_wide[i * TAPS + j, rows, :] = jnp.broadcast_to(one, (ROWS, 128))

    each(CHUNKS, spread, 0)

    load(5).wait()
    load(15).wait()
    fin_pad[...] = jnp.zeros_like(fin_pad)
    fin_pad[0:EMB, :] = fin_ref[...]
    fin_hi, fin_lo = split(fin_pad[...])
    fin_three = jnp.concatenate([fin_hi, fin_hi, fin_lo], axis=0)
    WIDE = 512

    def network(d):
        cols = pl.ds(d * WIDE, WIDE)
        f = feat[:, cols]
        pre = mm(fin_three, jnp.concatenate([f, f[0:FEAT, :]], axis=0), 0, 0)
        s, c = sin_cos(pre)
        bend[:, cols] = c
        a, b = split(s)
        act[0:FH, cols] = a
        act[FH : 2 * FH, cols] = b

    each(SEQ // WIDE, network, 0)

    tail_copy.wait_recv()
    inside = jnp.where(me > 0, 1.0, 0.0)
    prev[...] = (mm(tails_in[...], tail_sel[...], 0, 0) * inside).astype(bf16)

    def moved(x, by):
        return x if by == 0 else pltpu.roll(x, by, 1)

    def short(i, ref, rows):
        x = jnp.concatenate([prev[rows, i * 128 : (i + 1) * 128], ref[rows, :]], axis=1)
        acc = None
        for j in range(TAPS):
            y = moved(x, j)[:, 128:384]
            shifted[i * TAPS + j, rows, :] = y
            tap = tap_wide[i * TAPS + j, rows, :]
            term = jnp.concatenate([tap, tap], axis=1) * y.astype(f32)
            acc = term if acc is None else acc + term
        shorts[i, rows, :] = acc
        return acc

    def scatter(out, inn, send, recv):
        inn[me] = out[me]
        peers(lambda p: copy(out.at[p], inn.at[me], send.at[p], recv.at[me], at(p)).start())

    def short_part(which, out):
        for part in range(CHUNKS):
            rows = pl.ds(part * ROWS, ROWS)
            if which == 0:
                x = short(1, k_ref, rows) * short(2, v_ref, rows)
            else:
                x = cot_ref[rows, :].astype(f32) * short(0, q_ref, rows)
            for h in range(2):
                out[part * 2 + h] = x[h * 16 : (h + 1) * 16, :].astype(bf16)

    short_part(0, u_out)
    scatter(u_out, u_in, u_s, u_r)
    load(3).wait()
    short_part(1, g_out)
    scatter(g_out, g_in, g_s, g_r)

    for k in (6, 7, 8):
        load(k).wait()
    eye = (lax.broadcasted_iota(jnp.int32, (OWN, OWN), 0)
           == lax.broadcasted_iota(jnp.int32, (OWN, OWN), 1)).astype(f32)
    decay = jnp.sum(eye * decay_ref[...], axis=1, keepdims=True)
    skip = jnp.sum(eye * skip_ref[...], axis=1, keepdims=True)
    w_hi, w_lo = split(fout_ref[...])
    w_two = jnp.concatenate([w_hi, w_lo], axis=0)
    w_three = jnp.concatenate([w_hi, w_hi, w_lo], axis=0)
    scale = 1.0 / math.sqrt(SEQ)

    def filters(d):
        cols = pl.ds(d * WIDE, WIDE)
        raw = mm(w_two, act[0:FH, cols])
        raw = raw[0:OWN, :] + raw[OWN : 2 * OWN, :] + mm(w_hi, act[FH : 2 * FH, cols])
        t = (d * WIDE + lax.broadcasted_iota(jnp.int32, (OWN, WIDE), 1)).astype(f32)
        e = jnp.exp(-decay * (t * (1.0 / SEQ))) * scale
        h = raw * e
        for n in range(WIDE // 128):
            rows = pl.ds((d * (WIDE // 128) + n) * OWN, OWN)
            env[rows, :] = e[:, n * 128 : (n + 1) * 128]
            sig[rows, :] = h[:, n * 128 : (n + 1) * 128]

    each(SEQ // WIDE, filters, 0)

    for k in (9, 10, 11, 12, 13, 14):
        load(k).wait()
    GRP = 4
    tc, ts = twist[0:K1, :], twist[K1 : 2 * K1, :]

    def three(x, axis):
        hi, lo = split(x)
        return jnp.concatenate([hi, lo, hi], axis=axis)

    def forward(src, spec, exact):
        for grp in range(OWN // GRP):
            x = jnp.concatenate(
                [src[pl.ds(grp * GRP + c, BLK, stride=OWN), :] for c in range(GRP)], axis=1)
            if exact:
                x = x.astype(bf16)
                a = mm(c1_two[...], jnp.concatenate([x, x], axis=0))
            else:
                a = mm(c1_three[...], three(x, 0))
            re, im = [], []
            for c in range(GRP):
                ar = a[0:K1, c * 128 : (c + 1) * 128]
                ai = a[K1 : 2 * K1, c * 128 : (c + 1) * 128]
                re.append(ar * tc + ai * ts)
                im.append(ai * tc - ar * ts)
            x = jnp.concatenate([jnp.concatenate(re, 0), jnp.concatenate(im, 0)], axis=1)
            spec[grp * GRP * K1 : (grp + 1) * GRP * K1, :] = mm(three(x, 1), fwd_three[...])

    def backward(first, second, conj, dst):
        for grp in range(OWN // GRP):
            rows = slice(grp * GRP * K1, (grp + 1) * GRP * K1)
            ar, ai = first[rows, 0:128], first[rows, 128:256]
            br, bi = second[rows, 0:128], second[rows, 128:256]
            if conj:
                y = [ar * br + ai * bi, ai * br - ar * bi]
            else:
                y = [ar * br - ai * bi, ar * bi + ai * br]
            z = mm(three(jnp.concatenate(y, axis=1), 1), inv_three[...])
            out = []
            for c in range(GRP):
                zr = z[c * K1 : (c + 1) * K1, 0:128]
                zi = z[c * K1 : (c + 1) * K1, 128:256]
                out.append(jnp.concatenate([zr * tc - zi * ts, zi * tc + zr * ts], axis=0))
            r = mm(d1_three[...], three(jnp.concatenate(out, axis=1), 0))
            for c in range(GRP):
                dst[pl.ds(grp * GRP + c, BLK, stride=OWN), :] = r[:, c * 128 : (c + 1) * 128]

    forward(sig, spec_h, False)

    def wait_all(out, inn, send, recv):
        peers(lambda p: copy(out.at[p], inn.at[p], send.at[p], recv.at[p], at(p)).wait_recv())

    def unfold(inn, dst):
        for n in range(BLK):
            half = n % 2 * 128
            dst[n * 16 : (n + 1) * 16, :] = inn[n // 2, :, half : half + 128].astype(f32)

    def fold(result, direct, out):
        for s in range(NCTX):
            x = jnp.concatenate(
                [result[(2 * s + h) * 16 : (2 * s + h + 1) * 16, :] for h in range(2)], axis=1)
            out[s] = (x + skip * direct[s].astype(f32)).astype(bf16)

    wait_all(u_out, u_in, u_s, u_r)
    unfold(u_in, sig_u)
    forward(sig_u, spec_u, True)
    wait_all(g_out, g_in, g_s, g_r)
    unfold(g_in, sig)
    forward(sig, spec_g, True)

    backward(spec_g, spec_u, True, sig)
    sg_ref[...] = jnp.sum(eye * sig[0:16, 0:1], axis=0, keepdims=True) * scale
    store(7).start()
    for n in range(BLK):
        cols = slice(n * 128, (n + 1) * 128)
        a, b = split(sig[n * 16 : (n + 1) * 16, :] * env[n * 16 : (n + 1) * 16, :])
        bent[0:16, cols] = a
        bent[16:32, cols] = b
        bent[32:48, cols] = a
    def slopes(d):
        cols = pl.ds(d * 2 * WIDE, 2 * WIDE)
        a, b = split(mm(w_three, bent[:, cols], 0, 0) * bend[:, cols])
        slope[0:FH, cols] = a
        slope[FH : 2 * FH, cols] = b

    each(SEQ // (2 * WIDE), slopes, 0)
    total = mm(feat[...], slope[...], 1, 1)
    in_sum = (total[0:FEAT, :] + total[FEAT : 2 * FEAT, :] + pltpu.roll(total[0:FEAT, :], FH, 1))
    in_flat[...] = jnp.zeros_like(in_flat)
    in_flat[:, 0:FH] = in_sum[:, 0:FH]
    packed = in_flat[0:24, :] + pltpu.roll(in_flat[24:48, :], 64, 1)
    for k in range(3):
        in_tiles[k] = packed[k * 8 : (k + 1) * 8, :]

    def deal(go):
        for k in range(3):
            @pl.when(me != 2 * k + 1)
            def _(k=k):
                go(copy(in_tiles.at[k], in_parts.at[me], ip_s.at[k], ip_r.at[me], at(2 * k + 1)))

    deal(lambda c: c.start())
    backward(spec_u, spec_h, False, sig_u)
    fold(sig_u, u_in, conv_out)
    scatter(conv_out, conv_in, conv_s, conv_r)
    backward(spec_g, spec_h, True, sig)
    fold(sig, g_in, back_out)
    scatter(back_out, back_in, back_s, back_r)
    total = mm(bent[0:32, :], act[...], 1, 1)
    fog_ref[...] = (total[0:OWN, 0:FH] + total[OWN : 2 * OWN, 0:FH]
                    + pltpu.roll(total[0:OWN, :], FH, 1)[:, 0:FH]) * scale
    store(6).start()

    def take(i, g, rows):
        grads[i, rows, :] = g
        hi, lo = split(g[:, 0:128])
        ahead[rows, i * 256 : i * 256 + 128] = hi
        ahead[rows, i * 256 + 128 : i * 256 + 256] = lo
        for j in range(TAPS):
            x = g * shifted[i * TAPS + j, rows, :].astype(f32)
            hi, lo = split(x[:, 0:128] + x[:, 128:256])
            prods[i * TAPS + j, rows, 0:128] = hi
            prods[i * TAPS + j, rows, 128:256] = lo

    pick_row = lax.broadcasted_iota(jnp.int32, (16, 256), 0)

    def tap_sum(k, which):
        total = jnp.zeros((16, 256), f32)
        for n, i in enumerate(which):
            for j in range(TAPS):
                pick = (pick_row == n * 8 + j).astype(f32).astype(bf16)
                total = total + mm(pick, prods[i * TAPS + j], 1, 1)
        tap_out[k] = total.astype(bf16)
        tap_in[k, me] = tap_out[k]
        peers(lambda p: copy(tap_out.at[k], tap_in.at[k, me], tp_s.at[k, p], tp_r.at[k, me],
                             at(p)).start())

    def conv_part(d):
        rows = pl.ds(d * ROWS, ROWS)
        cv = jnp.concatenate([conv_in[2 * d], conv_in[2 * d + 1]], axis=0).astype(f32)
        mixed_ref[rows, :] = (shorts[0, rows, :] * cv).astype(bf16)
        take(0, cot_ref[rows, :].astype(f32) * cv, rows)

    def back_part(d):
        rows = pl.ds(d * ROWS, ROWS)
        bk = jnp.concatenate([back_in[2 * d], back_in[2 * d + 1]], axis=0).astype(f32)
        take(1, bk * shorts[2, rows, :], rows)
        take(2, bk * shorts[1, rows, :], rows)

    wait_all(conv_out, conv_in, conv_s, conv_r)
    each(CHUNKS, conv_part, 0)
    store(0).start()
    tap_sum(0, (0,))

    @pl.when(in_owner)
    def _():
        peers(lambda p: copy(in_tiles.at[0], in_parts.at[p], ip_r.at[p], ip_r.at[p],
                             at(p)).wait_recv())
        in_parts[me] = in_tiles[in_index]
        t = in_parts[0]
        for p in range(1, NCTX):
            t = t + in_parts[p]
        in_row[ch] = t
        chan_peers(lambda n, p: copy(in_row.at[ch], in_row.at[ch], iq_s.at[n], iq_r.at[ch],
                                     over(p)).start())

    load(17).wait()
    load(18).wait()
    wait_all(back_out, back_in, back_s, back_r)
    each(CHUNKS, back_part, 0)
    tap_sum(1, (1, 2))
    heads_out[...] = mm(head_sel[...], ahead[...], 1, 1).astype(bf16)
    head_copy = copy(heads_out, heads_in, halo_s.at[1], halo_r.at[1], at(other(NCTX - 1)))
    head_copy.start()

    head_copy.wait_recv()
    before_end = jnp.where(me < NCTX - 1, 1.0, 0.0)
    after[...] = mm(heads_in[...], head_place[...], 0, 0) * before_end
    lane = lax.broadcasted_iota(jnp.int32, (ROWS, 128), 1)

    def proj(i, ref):
        def proj_part(d):
            rows = slice(d * ROWS, (d + 1) * ROWS)
            left, right = grads[i, rows, 0:128], grads[i, rows, 128:256]
            tap = tap_wide[i * TAPS, rows, :]
            acc = [tap * left, tap * right]
            for j in range(1, TAPS):
                tap = tap_wide[i * TAPS + j, rows, :]
                near, far = pltpu.roll(left, 128 - j, 1), pltpu.roll(right, 128 - j, 1)
                edge = after[rows, (i * 6 + j - 1) * 128 : (i * 6 + j) * 128]
                here = lane < 128 - j
                acc[0] = acc[0] + tap * jnp.where(here, near, far)
                acc[1] = acc[1] + tap * jnp.where(here, far, edge)
            ref[rows, 0:128] = acc[0].astype(bf16)
            ref[rows, 128:256] = acc[1].astype(bf16)

        for d in range(CHUNKS):
            proj_part(d)
        store(1 + i).start()

    proj(0, qg_ref)
    proj(1, kg_ref)
    proj(2, vg_ref)

    @pl.when(in_owner)
    def _():
        chan_peers(lambda n, p: copy(in_row.at[p], in_row.at[p], iq_s.at[n], iq_r.at[p],
                                     over(p)).wait_recv())
        t = in_row[0]
        for p in range(1, chans):
            t = t + in_row[p]
        in_sums[in_index] = t
        peers(lambda p: copy(in_sums.at[in_index], in_sums.at[in_index], is_s.at[p],
                             is_r.at[in_index], at(p)).start())

    for k in range(2):
        peers(lambda p: copy(tap_out.at[k], tap_in.at[k, p], tp_s.at[k, p], tp_r.at[k, p],
                             at(p)).wait_recv())
        t = tap_in[k, 0].astype(f32)
        for p in range(1, NCTX):
            t = t + tap_in[k, p].astype(f32)
        if k == 0:
            tg_ref[0] = t[0:TAPS, :] * scale
        else:
            tg_ref[1] = t[0:TAPS, :] * scale
            tg_ref[2] = t[8 : 8 + TAPS, :] * scale
    store(4).start()
    for k in range(3):
        @pl.when(me != 2 * k + 1)
        def _(k=k):
            copy(in_sums.at[k], in_sums.at[k], is_s.at[0], is_r.at[k], at(2 * k + 1)).wait_recv()
    sums = jnp.concatenate([in_sums[k] for k in range(3)], axis=0) * (scale / math.sqrt(D))
    fig_ref[0:24, :] = sums[:, 0:FH]
    fig_ref[24:EMB, :] = pltpu.roll(sums, 64, 1)[0 : EMB - 24, 0:FH]
    store(5).start()

    for k in range(8):
        store(k).wait()
    tail_copy.wait_send()
    head_copy.wait_send()
    deal(lambda c: c.wait_send())

    def left(p):
        for out, inn, send, recv in ((u_out, u_in, u_s, u_r), (g_out, g_in, g_s, g_r),
                                     (conv_out, conv_in, conv_s, conv_r),
                                     (back_out, back_in, back_s, back_r)):
            copy(out.at[p], inn.at[me], send.at[p], recv.at[me], at(p)).wait_send()
        for k in range(2):
            copy(tap_out.at[k], tap_in.at[k, me], tp_s.at[k, p], tp_r.at[k, me], at(p)).wait_send()

    peers(left)

    @pl.when(in_owner)
    def _():
        chan_peers(lambda n, p: copy(in_row.at[ch], in_row.at[ch], iq_s.at[n], iq_r.at[ch],
                                     over(p)).wait_send())
        peers(lambda p: copy(in_sums.at[in_index], in_sums.at[in_index], is_s.at[p],
                             is_r.at[in_index], at(p)).wait_send())


def hand_on(*refs):
    held, load_s, store_s = refs[16:24], refs[24], refs[25]
    loads = [pltpu.make_async_copy(refs[k], held[k], load_s.at[k]) for k in range(8)]
    stores = [pltpu.make_async_copy(held[k], refs[8 + k], store_s.at[k]) for k in range(8)]
    for c in loads:
        c.start()
    for k in range(8):
        loads[k].wait()
        stores[k].start()
    for c in stores:
        c.wait()


def per_device(consts, chans, query_proj, key_proj, value_proj, out_cotangent, short_taps,
               filter_in, filter_out, decay_rate, skip_gain):
    block = jax.ShapeDtypeStruct((256, POS), bf16)
    dma = pltpu.SemaphoreType.DMA
    V = pltpu.VMEM
    args = [query_proj, key_proj, value_proj, out_cotangent, short_taps, filter_in, filter_out.T,
            decay_rate.reshape(1, OWN), skip_gain.reshape(1, OWN)]
    args += [jnp.asarray(c) for c in consts]
    shapes = (block, block, block, block,
              jax.ShapeDtypeStruct((3, TAPS, 256), f32),
              jax.ShapeDtypeStruct((EMB, FH), f32),
              jax.ShapeDtypeStruct((OWN, FH), f32),
              jax.ShapeDtypeStruct((1, OWN), f32))
    hbm = pl.BlockSpec(memory_space=pl.ANY)
    outs = pl.pallas_call(
        functools.partial(kernel, chans),
        out_shape=shapes,
        in_specs=[hbm] * LOADS,
        out_specs=[hbm] * 8,
        scratch_shapes=[V(a.shape, a.dtype) for a in args] + [V(a.shape, a.dtype) for a in shapes] + [
            dma((LOADS,)), dma((8,)),
            V((32, 256), bf16), V((32, 256), bf16), V((48, 256), bf16), V((48, 256), bf16),
            V((24, 256), f32), V((256, 128), f32), V((FEAT, FH), f32),
            V((21, 256, 128), f32), V((256, 384), bf16), V((256, 18 * 128), f32),
            V((3, 256, 256), f32), V((21, 256, 256), bf16),
            V((3, 256, 256), f32), V((256, 768), bf16), V((FH, SEQ), f32),
            V((2 * FH, SEQ), bf16), V((512, 128), f32),
            V((512, 128), f32), V((512, 128), f32),
            V((OWN * K1, 256), f32), V((OWN * K1, 256), f32), V((OWN * K1, 256), f32),
            V((NCTX, 16, 256), bf16), V((NCTX, 16, 256), bf16),
            V((NCTX, 16, 256), bf16), V((NCTX, 16, 256), bf16),
            V((NCTX, 16, 256), bf16), V((NCTX, 16, 256), bf16),
            V((NCTX, 16, 256), bf16), V((NCTX, 16, 256), bf16),
            V((3 * OWN, SEQ), bf16), V((2 * FH, SEQ), bf16),
            V((21, 256, 256), bf16), V((2, 16, 256), bf16), V((2, NCTX, 16, 256), bf16),
            V((3, 8, 128), f32), V((NCTX, 8, 128), f32), V((chans, 8, 128), f32),
            V((3, 8, 128), f32), V((48, 128), f32),
            dma((2,)), dma((2,)), dma((NCTX,)), dma((NCTX,)), dma((NCTX,)), dma((NCTX,)),
            dma((NCTX,)), dma((NCTX,)), dma((NCTX,)), dma((NCTX,)),
            dma((2, NCTX)), dma((2, NCTX)), dma((3,)), dma((NCTX,)),
            dma((chans,)), dma((chans,)), dma((NCTX,)), dma((3,)),
        ],
        compiler_params=pltpu.CompilerParams(
            collective_id=0, has_side_effects=True, vmem_limit_bytes=56 * 1024 * 1024),
    )(*args)
    outs = pl.pallas_call(
        hand_on,
        out_shape=shapes,
        in_specs=[hbm] * 8,
        out_specs=[hbm] * 8,
        scratch_shapes=[V(a.shape, a.dtype) for a in shapes] + [dma((8,)), dma((8,))],
    )(*outs)
    return outs[:6] + (outs[6].T, outs[7].reshape(OWN))


def solution(mesh):
    consts = tables()
    return jax.shard_map(
        functools.partial(per_device, consts, mesh.shape["chan"]),
        mesh=mesh,
        in_specs=(
            P("chan", "ctx"),
            P("chan", "ctx"),
            P("chan", "ctx"),
            P("chan", "ctx"),
            P(None, None, "chan"),
            P(),
            P(None, ("chan", "ctx")),
            P(("chan", "ctx")),
            P(("chan", "ctx")),
        ),
        out_specs=(
            P("chan", "ctx"),
            P("chan", "ctx"),
            P("chan", "ctx"),
            P("chan", "ctx"),
            P(None, None, "chan"),
            P(),
            P(None, ("chan", "ctx")),
            P(("chan", "ctx")),
        ),
        check_vma=False,
    )
```
